256 devices in a mesh: dap: 128 (over x_lo, y, z, core), heads: 2 (over x_hi).
Axes of the slice: x: 4 (x_hi: 2, x_lo: 2; x = x_hi * 2 + x_lo), y: 4, z: 8, core: 2. Of those that a mesh axis runs over, the one named last changes fastest.
Arguments:
- pair: bfloat16 [768, 768, 128], P('dap'), may hold values from -6 to 6
- ln_gain: float32 [128], replicated, may hold values from 0.1 to 1.9
- ln_shift: float32 [128], replicated, may hold values from -3 to 3
- w_project: bfloat16 [128, 4, 128], P(None, None, 'heads'), may hold values from -0.5 to 0.5
- w_bias: bfloat16 [128, 4], P(None, 'heads'), may hold values from -2 to 2
- w_out: bfloat16 [128, 128], P('heads'), may hold values from -0.5 to 0.5
Outputs:
- update: bfloat16 [768, 768, 128], P(('dap', 'heads'))
The draws below stay inside these ranges and needn't reach their ends.
All inputs are finite; a program needn't handle non-finite values.
Results may differ from the reference program's by a relative error of at most 0.0039.
The reference program's roundings to bfloat16 on the way (of `normed`, `queries`, `gating`, `weights` and `gated_out`) count: a program that leaves them out, or rounds other values in their place, can miss the bound.
Values may be sent and summed in bfloat16 or wider, within the bound.
No kernel may reach another device: no remote copies, remote signals or barrier semaphores. Data moves between devices by JAX's collectives and lax.ppermute only.
A program may use at most 64 MiB of HBM per device.

```python
import math
import jax
import jax.numpy as jnp
from jax import lax

C = 128
H = 4
DH = 32
N = 768


def draw_w_bias(key, part):
    key = jax.random.fold_in(key, 11)
    values = jnp.clip(jax.random.normal(key, (C, H), jnp.float32), -4.0, 4.0) * 0.0625
    return values.astype(jnp.bfloat16)


def steps_of(stream_key, extent, shards, low, largest):
    def one(dim, blocks):
        heights = jax.random.uniform(jax.random.fold_in(jax.random.fold_in(stream_key, 6), dim), (blocks,), jnp.float32, low / len(shards), largest / len(shards))
        return jnp.repeat(jnp.exp(heights), extent[dim] // blocks).reshape((-1,) + (1,) * (len(extent) - dim - 1))

    gain = one(*shards[0])
    for cut in shards[1:]:
        gain = gain * one(*cut)
    return gain


def scatter_about(stream_key, shape, width, reach, pieces=(), held_as=jnp.bfloat16):
    loudness = steps_of(stream_key, shape, pieces, -0.22, 0.18) if pieces else 1.0
    entries = jax.random.normal(stream_key, shape, jnp.float32) * width * loudness
    return jnp.minimum(jnp.maximum(entries, -reach), reach).astype(held_as)


def setup_inputs(seed: int = 0) -> dict:
    seeds = jax.random.split(jax.random.key(seed), 7)
    return {
        "pair": scatter_about(seeds[0], (N, N, C), 1.0, 6.0, ((0, 128),)),
        "ln_gain": jnp.clip(1.0 + 0.18 * jax.random.normal(seeds[1], (C,), jnp.float32), 0.1, 1.9),
        "ln_shift": scatter_about(seeds[2], (C,), 0.5, 3.0, (), jnp.float32),
        "w_project": scatter_about(seeds[3], (C, 4, H * DH), C ** -0.5, 0.5, ((2, 2),)),
        "w_bias": draw_w_bias(jax.random.fold_in(seeds[6], 71), 0),
        "w_out": scatter_about(seeds[5], (H * DH, C), (H * DH) ** -0.5, 0.5, ((0, 2),)),
    }


def normalize(pair, ln_gain, ln_shift):
    values_f = pair.astype(jnp.float32)
    average = lax.optimization_barrier(jnp.mean(values_f, axis=-1, keepdims=True))
    centred = values_f - average
    variance = lax.optimization_barrier(jnp.mean(centred * centred, axis=-1, keepdims=True))
    return (centred * lax.rsqrt(variance + 1e-05) * ln_gain + ln_shift).astype(jnp.bfloat16)

def project_entries(normed, flat_w):
    projected = jnp.dot(normed, flat_w, preferred_element_type=jnp.float32)
    head_width = flat_w.shape[1] // 4
    head_part = projected[..., :3 * head_width].astype(jnp.bfloat16)
    gating = jax.nn.sigmoid(projected[..., 3 * head_width:]).astype(jnp.bfloat16)
    return jnp.concatenate([head_part, gating], axis=-1)

def reference(pair, ln_gain, ln_shift, w_project, w_bias, w_out):
    normed = normalize(pair, ln_gain, ln_shift)
    pair_bias = jnp.einsum('abc,ch->hab', normed.astype(jnp.float32), w_bias.astype(jnp.float32))
    bias_key_last = jnp.swapaxes(pair_bias, 1, 2)
    flat_w = w_project.reshape(C, 4 * H * DH)
    col_block = 8

    def one_block(first_col):
        columns = lax.dynamic_slice_in_dim(normed, first_col, col_block, 1)
        packed = project_entries(columns, flat_w).reshape(N, col_block, 4, H, DH)
        queries = packed[:, :, 0].astype(jnp.float32)
        keys_all = packed[:, :, 1].astype(jnp.float32)
        values = packed[:, :, 2].astype(jnp.float32)
        gating = packed[:, :, 3].astype(jnp.float32)
        scores = jnp.einsum('ibhc,kbhc->bhik', queries, keys_all) * (1.0 / math.sqrt(DH)) + bias_key_last[None]
        highest = lax.optimization_barrier(jnp.max(scores, axis=-1, keepdims=True))
        exponent = jnp.exp(scores - highest)
        totals = lax.optimization_barrier(jnp.sum(exponent, axis=-1))
        weights = exponent.astype(jnp.bfloat16)
        attended = jnp.einsum('bhik,kbhc->ibhc', weights.astype(jnp.float32), values)
        attended = attended / jnp.transpose(totals, (2, 0, 1))[..., None]
        gated_out = (attended * gating).astype(jnp.bfloat16).reshape(N * col_block, H * DH)
        return jnp.dot(gated_out, w_out, preferred_element_type=jnp.float32).astype(jnp.bfloat16).reshape(N, col_block, C)
    starts = jnp.arange(0, N, col_block, dtype=jnp.int32)
    stacked = lax.map(one_block, starts)
    return jnp.transpose(stacked, (1, 0, 2, 3)).reshape(N, N, C)
```

```python
import functools
import math

import jax
import jax.numpy as jnp
from jax import lax
from jax.experimental import pallas as pl
from jax.experimental.pallas import tpu as pltpu
from jax.sharding import Mesh
from jax.sharding import PartitionSpec as P

F32 = jnp.float32
BF16 = jnp.bfloat16
CHIP = ("xl", "y", "z")
DAP = ("xl", "y", "z", "c")
N, C, H, DH = 768, 128, 4, 32
CHIPS, COLS, ROWS = 64, 12, 6
QR = 3 * CHIPS
KH = ROWS * CHIPS
PIECE = 40
ROOT = math.sqrt(DH)
NT = (((1,), (1,)), ((), ()))


def params(mb):
    return pltpu.CompilerParams(vmem_limit_bytes=mb * 2**20)


def norm_kernel(pair_ref, gain_ref, shift_ref, rows_ref, split_ref, held):
    x = pair_ref[0].astype(F32)
    average = jnp.mean(x, axis=-1, keepdims=True)
    centred = x - average
    variance = jnp.mean(centred * centred, axis=-1, keepdims=True)
    normed = (centred * lax.rsqrt(variance + 1e-05) * gain_ref[...] + shift_ref[...]).astype(BF16)
    rows_ref[0] = normed
    held[...] = normed.astype(F32)
    for m in range(COLS):
        split_ref[0, m] = held[pl.ds(m, CHIPS, stride=COLS), :].astype(BF16)


def normalize(pair, gain, shift):
    return pl.pallas_call(
        norm_kernel,
        grid=(ROWS,),
        in_specs=[
            pl.BlockSpec((1, N, C), lambda a: (a, 0, 0)),
            pl.BlockSpec((1, C), lambda a: (0, 0)),
            pl.BlockSpec((1, C), lambda a: (0, 0)),
        ],
        out_specs=[
            pl.BlockSpec((1, N, C), lambda a: (a, 0, 0)),
            pl.BlockSpec((1, COLS, CHIPS, C), lambda a: (a, 0, 0, 0)),
        ],
        out_shape=[
            jax.ShapeDtypeStruct((ROWS, N, C), BF16),
            jax.ShapeDtypeStruct((ROWS, COLS, CHIPS, C), BF16),
        ],
        scratch_shapes=[pltpu.VMEM((N, C), F32)],
        compiler_params=params(24),
        name="norm",
    )(pair, gain, shift)


def bias_kernel(head_ref, split_ref, own_ref, other_ref, out_ref):
    for a in range(ROWS):
        entries = split_ref[a, :, 0].reshape(2 * QR, C)
        own = lax.dot_general(own_ref[...], entries, NT, preferred_element_type=F32) * ROOT
        other = lax.dot_general(other_ref[...], entries, NT, preferred_element_type=F32) * ROOT
        for core in range(2):
            at = core * QR
            row = jnp.concatenate(
                [part[g : g + 1, at : at + QR] for part in (own, other) for g in range(2)], axis=1
            )
            for s in range(6):
                out_ref[core, a * 6 + s : a * 6 + s + 1, :] = row[:, s * C : (s + 1) * C]
    out_ref[:, 36:, :] = jnp.zeros((2, PIECE - 36, C), F32)


def bias_pieces(head, split, own, other):
    return pl.pallas_call(
        bias_kernel,
        grid_spec=pltpu.PrefetchScalarGridSpec(
            num_scalar_prefetch=1,
            grid=(1,),
            in_specs=[
                pl.BlockSpec((ROWS, 2, 1, QR, C), lambda g, head: (0, 0, head[0], 0, 0)),
                pl.BlockSpec((16, C), lambda g, head: (0, 0)),
                pl.BlockSpec((16, C), lambda g, head: (0, 0)),
            ],
            out_specs=pl.BlockSpec((2, PIECE, C), lambda g, head: (0, 0, 0)),
        ),
        out_shape=jax.ShapeDtypeStruct((2, PIECE, C), F32),
        compiler_params=params(24),
        name="bias",
    )(head, split.reshape(ROWS, 2, 2, QR, C), own, other)


def place_kernel(where_ref, *refs):
    parts, out_ref = refs[:4], refs[4]
    y, core = where_ref[0], where_ref[1]
    for step, part in enumerate(parts):
        source = lax.rem(y - step + 4, 4)
        for other in range(2):
            from_core = lax.rem(core + other, 2)
            for a in range(ROWS):
                for xl in range(2):
                    to = (other * ROWS + a) * CHIPS + xl * 32 + source * 8
                    to = pl.multiple_of(to, 8)
                    for s in range(6):
                        at = xl * 16 * PIECE + from_core * PIECE + a * 6 + s
                        out_ref[pl.ds(to, 8), s * C : (s + 1) * C] = part[
                            pl.ds(at, 8, stride=2 * PIECE), :
                        ]


def place_bias(where, parts):
    return pl.pallas_call(
        place_kernel,
        grid_spec=pltpu.PrefetchScalarGridSpec(
            num_scalar_prefetch=1,
            grid=(1,),
            in_specs=[pl.BlockSpec((32 * PIECE, C), lambda g, w: (0, 0))] * 4,
            out_specs=pl.BlockSpec((N, 4 * QR), lambda g, w: (0, 0)),
        ),
        out_shape=jax.ShapeDtypeStruct((N, 4 * QR), F32),
        compiler_params=params(32),
        name="place",
    )(where, *parts)


def attend_kernel(
    head_ref, own_ref, other_ref, query_ref, bias_ref, wk_ref, wv_ref, wq_ref, wg_ref, wo_ref, out_ref
):
    entries = jnp.concatenate([own_ref[0], other_ref[0]], axis=0)
    asked = jnp.concatenate([query_ref[0], query_ref[0]], axis=0)
    keys = jnp.dot(entries, wk_ref[...], preferred_element_type=F32).astype(BF16)
    values = lax.dot_general(wv_ref[...], entries, NT, preferred_element_type=F32).astype(BF16)
    queries = lax.dot_general(wq_ref[...], asked, NT, preferred_element_type=F32)
    gates = jax.nn.sigmoid(lax.dot_general(wg_ref[...], asked, NT, preferred_element_type=F32))
    gates = gates.astype(BF16).astype(F32)
    head_of_channel = lax.broadcasted_iota(jnp.int32, (C, 2 * QR), 0) // DH
    second = (lax.broadcasted_iota(jnp.int32, (C, 2 * QR), 1) >= QR).astype(jnp.int32)
    masked = [jnp.where(head_of_channel == 2 * g + second, queries, 0.0).astype(BF16) for g in range(2)]
    masked = jnp.concatenate(masked, axis=1)
    factor = 1.0 / (ROOT * math.log(2.0))
    sums, totals = [], []
    for n in range(3):
        lanes = slice(n * 256, (n + 1) * 256)
        scores = jnp.dot(keys, masked[:, lanes], preferred_element_type=F32) + bias_ref[:, lanes]
        highest = jnp.max(scores, axis=0, keepdims=True)
        exponent = jnp.exp2((scores - highest) * factor)
        totals.append(jnp.sum(exponent, axis=0, keepdims=True))
        sums.append(jnp.dot(values, exponent.astype(BF16), preferred_element_type=F32))
    sums = jnp.concatenate(sums, axis=1)
    totals = jnp.concatenate(totals, axis=1)
    first = lax.broadcasted_iota(jnp.int32, (DH, 2 * QR), 1) < QR
    gated = []
    for g in range(2):
        lanes = slice(g * 2 * QR, (g + 1) * 2 * QR)
        low, high = slice(2 * g * DH, (2 * g + 1) * DH), slice((2 * g + 1) * DH, (2 * g + 2) * DH)
        attended = jnp.where(first, sums[low, lanes], sums[high, lanes]) / totals[:, lanes]
        gated.append(attended * jnp.where(first, gates[low], gates[high]))
    gated = jnp.concatenate(gated, axis=0)
    turned = gated.T.astype(BF16)
    turned = jnp.concatenate([turned[:QR], turned[QR:]], axis=1)
    update = jnp.dot(turned, wo_ref[...], preferred_element_type=F32).astype(BF16)
    out_ref[0] = update


def attend(head, own, other, bias, wk, wv, wq, wg, wo):
    weight = pl.BlockSpec((C, C), lambda m, head: (0, 0))
    return pl.pallas_call(
        attend_kernel,
        grid_spec=pltpu.PrefetchScalarGridSpec(
            num_scalar_prefetch=1,
            grid=(COLS,),
            in_specs=[
                pl.BlockSpec((1, KH, C), lambda m, head: (m, 0, 0)),
                pl.BlockSpec((1, KH, C), lambda m, head: (m, 0, 0)),
                pl.BlockSpec((1, QR, C), lambda m, head: (m, head[0], 0)),
                pl.BlockSpec((N, 4 * QR), lambda m, head: (0, 0)),
                weight,
                weight,
                weight,
                weight,
                weight,
            ],
            out_specs=pl.BlockSpec((1, QR, C), lambda m, head: (m, 0, 0)),
        ),
        out_shape=jax.ShapeDtypeStruct((COLS, QR, C), BF16),
        compiler_params=params(48),
        name="attend",
    )(head, own, other, own, bias, wk, wv, wq, wg, wo)


def local(pair, ln_gain, ln_shift, w_project, w_bias, w_out):
    swap_heads = functools.partial(lax.ppermute, axis_name="h", perm=[(0, 1), (1, 0)])
    swap_cores = functools.partial(lax.ppermute, axis_name="c", perm=[(0, 1), (1, 0)])
    head = lax.axis_index("h").astype(jnp.int32).reshape(1)
    where = jnp.stack([lax.axis_index("y"), lax.axis_index("c")]).astype(jnp.int32)

    bias_own = jnp.pad(w_bias.T, ((0, 14), (0, 0)))
    bias_other = swap_heads(bias_own)
    weights = jnp.concatenate([w_project.reshape(C, 4 * 64), w_out.T], axis=1)
    weights_other = swap_heads(weights)

    rows, split = normalize(pair, ln_gain.reshape(1, C), ln_shift.reshape(1, C))
    pieces = bias_pieces(head, split, bias_own, bias_other)
    spread = jnp.broadcast_to(pieces[None], (16, 2, PIECE, C)).reshape(32, PIECE, C)
    near = lax.all_to_all(spread, ("xl", "z", "c"), 0, 0, tiled=True)
    parts = [near] + [lax.ppermute(near, "y", [(i, (i + o) % 4) for i in range(4)]) for o in (1, 2, 3)]
    bias = place_bias(where, [part.reshape(32 * PIECE, C) for part in parts])

    blocks = rows.reshape(ROWS, CHIPS, COLS, C).transpose(1, 0, 2, 3).reshape(CHIPS, ROWS * COLS, C)
    arrived = lax.all_to_all(blocks, CHIP, 0, 0, tiled=True)
    own = arrived.reshape(CHIPS, ROWS, COLS, C).transpose(2, 1, 0, 3).reshape(COLS, KH, C)
    other = swap_cores(own)

    full = [
        jnp.concatenate([weights[:, t * 64 : (t + 1) * 64], weights_other[:, t * 64 : (t + 1) * 64]], axis=1)
        for t in range(5)
    ]
    wo = full[4].T.reshape(2, 2, DH, C).transpose(1, 0, 2, 3).reshape(C, C)
    done = attend(head, own, other, bias, full[1], full[2].T, full[0].T, full[3].T, wo)

    sent = done.reshape(COLS, 3, CHIPS, C).transpose(2, 1, 0, 3).reshape(CHIPS, 3 * COLS, C)
    returned = lax.all_to_all(sent, CHIP, 0, 0, tiled=True)
    return returned.reshape(CHIPS, 3, COLS, C).transpose(1, 0, 2, 3).reshape(3, N, C)


def solution(mesh):
    fine = Mesh(mesh.devices.reshape(2, 4, 8, 2, 2), DAP + ("h",))
    in_specs = (P(DAP, None, None), P(), P(), P(None, None, "h"), P(None, "h"), P("h", None))
    out_specs = P(DAP + ("h",), None, None)
    return jax.shard_map(local, mesh=fine, in_specs=in_specs, out_specs=out_specs, check_vma=False)
```

```python
import functools
import math

import jax
import jax.numpy as jnp
from jax import lax
from jax.experimental import pallas as pl
from jax.experimental.pallas import tpu as pltpu
from jax.sharding import Mesh
from jax.sharding import PartitionSpec as P

F32 = jnp.float32
BF16 = jnp.bfloat16
CHIP = ("xl", "y", "z")
DAP = ("xl", "y", "z", "c")
N, C, H, DH = 768, 128, 4, 32
CHIPS, COLS, ROWS = 64, 12, 6
QR = 3 * CHIPS
KH = ROWS * CHIPS
LEVELS = 240
GROUP = 6
PIECE = 36
ROOT = math.sqrt(DH)
NT = (((1,), (1,)), ((), ()))


def params(mb):
    return pltpu.CompilerParams(vmem_limit_bytes=mb * 2**20)


def layer_norm(x, gain, shift):
    average = jnp.mean(x, axis=-1, keepdims=True)
    centred = x - average
    variance = jnp.mean(centred * centred, axis=-1, keepdims=True)
    return centred * lax.rsqrt(variance + 1e-05) * gain + shift


def norm_kernel(pair_ref, gain_ref, shift_ref, out_ref):
    out_ref[0] = layer_norm(pair_ref[0].astype(F32), gain_ref[...], shift_ref[...]).astype(BF16)


def normalize(pair, gain, shift):
    return pl.pallas_call(
        norm_kernel,
        grid=(ROWS,),
        in_specs=[
            pl.BlockSpec((1, N, C), lambda a: (a, 0, 0)),
            pl.BlockSpec((1, C), lambda a: (0, 0)),
            pl.BlockSpec((1, C), lambda a: (0, 0)),
        ],
        out_specs=pl.BlockSpec((1, N, C), lambda a: (a, 0, 0)),
        out_shape=jax.ShapeDtypeStruct((ROWS, N, C), BF16),
        compiler_params=params(24),
        cost_estimate=pl.CostEstimate(flops=10 * ROWS * N * C, bytes_accessed=4 * ROWS * N * C, transcendentals=0),
        name="norm",
    )(pair, gain, shift)


def bias_range(w, gain, shift):
    w = w.astype(F32)
    middle = jnp.sum(w * shift, axis=1, keepdims=True)
    reach = jnp.sqrt(C * jnp.sum(w * w * gain * gain, axis=1, keepdims=True))
    rounded = jnp.sum(jnp.abs(w * shift), axis=1, keepdims=True)
    return middle, reach * (1 + 1 / 256) + rounded / 256 + 1e-20


def encode(x):
    size = jnp.minimum(jnp.abs(x) * LEVELS, LEVELS - 0.01)
    whole = jnp.floor(size)
    code = jnp.exp2(whole - LEVELS / 2) * (1 + (size - whole))
    return jnp.where(x < 0, -code, code).astype(BF16)


def decode(code):
    code = code.astype(F32)
    size = jnp.abs(code)
    whole = jnp.floor(jnp.log2(size))
    x = (whole + (LEVELS / 2 - 1) + size * jnp.exp2(-whole)) / LEVELS
    return jnp.where(code < 0, -x, x)


def bias_kernel(
    where_ref, own_ref, other_ref, gain_ref, shift_ref, w_own_ref, w_other_ref, out_ref, held, coded
):
    first = 6 * where_ref[1] + 3 * where_ref[0]
    weights = [w_ref[...] for w_ref in (w_own_ref, w_other_ref)]
    ranges = [bias_range(w, gain_ref[...], shift_ref[...]) for w in weights]
    for o, rows_ref in enumerate((own_ref, other_ref)):
        for a in range(ROWS):
            held[...] = rows_ref[a].astype(F32)
            entries = jnp.concatenate(
                [held[pl.ds(first + r, CHIPS, stride=COLS), :] for r in range(3)], axis=0
            )
            entries = layer_norm(entries, gain_ref[...], shift_ref[...]).astype(BF16)
            parts = [
                (lax.dot_general(w, entries, NT, preferred_element_type=F32) - middle) / reach
                for w, (middle, reach) in zip(weights, ranges)
            ]
            row = jnp.concatenate([part[g : g + 1] for part in parts for g in range(2)], axis=1)
            for s in range(6):
                at = (o * ROWS + a) * 6 + s
                coded[at : at + 1, :] = row[:, s * C : (s + 1) * C]
    out_ref[...] = encode(coded[...])


def bias_piece(where, own, other, gain, shift, w_own, w_other):
    return pl.pallas_call(
        bias_kernel,
        grid_spec=pltpu.PrefetchScalarGridSpec(
            num_scalar_prefetch=1,
            grid=(1,),
            in_specs=[pl.BlockSpec((ROWS, N, C), lambda g, w: (0, 0, 0))] * 2
            + [pl.BlockSpec((1, C), lambda g, w: (0, 0))] * 2
            + [pl.BlockSpec((16, C), lambda g, w: (0, 0))] * 2,
            out_specs=pl.BlockSpec((2 * PIECE, C), lambda g, w: (0, 0)),
            scratch_shapes=[pltpu.VMEM((N, C), F32), pltpu.VMEM((2 * PIECE, C), F32)],
        ),
        out_shape=jax.ShapeDtypeStruct((2 * PIECE, C), BF16),
        compiler_params=params(24),
        cost_estimate=pl.CostEstimate(flops=40 * N * ROWS * C, bytes_accessed=4 * ROWS * N * C, transcendentals=0),
        name="bias",
    )(where, own, other, gain, shift, w_own, w_other)


def place_kernel(where_ref, gain_ref, shift_ref, w_own_ref, w_other_ref, *refs):
    parts, out_ref, held = refs[:4], refs[4], refs[5]
    y, xl, z = where_ref[2], where_ref[3], where_ref[4]
    turn = lax.rem(z + 4, 8)
    reaches = [bias_range(w_ref[...], gain_ref[...], shift_ref[...])[1] for w_ref in (w_own_ref, w_other_ref)]
    scale = [jnp.broadcast_to(reach[g : g + 1] * ROOT, (8, QR)) for reach in reaches for g in range(2)]
    scale = jnp.concatenate(scale, axis=1)
    for step, part in enumerate(parts):
        source = lax.rem(y - step + 4, 4)
        held[...] = decode(part[...])
        for step_x in range(2):
            from_x = lax.rem(xl + step_x, 2)
            for other in range(2):
                for a in range(ROWS):
                    to = (other * ROWS + a) * CHIPS + from_x * 32 + source * 8
                    to = pl.multiple_of(to, 8)
                    for s in range(6):
                        at = step_x * 16 * PIECE + other * PIECE + a * 6 + s
                        lanes = slice(s * C, (s + 1) * C)
                        ring = held[pl.ds(at, 8, stride=2 * PIECE), :]
                        out_ref[pl.ds(to, 8), lanes] = pltpu.roll(ring, turn, 0) * scale[:, lanes]


def place_bias(where, gain, shift, w_own, w_other, parts):
    return pl.pallas_call(
        place_kernel,
        grid_spec=pltpu.PrefetchScalarGridSpec(
            num_scalar_prefetch=1,
            grid=(1,),
            in_specs=[pl.BlockSpec((1, C), lambda g, w: (0, 0))] * 2
            + [pl.BlockSpec((16, C), lambda g, w: (0, 0))] * 2
            + [pl.BlockSpec((32 * PIECE, C), lambda g, w: (0, 0))] * 4,
            out_specs=pl.BlockSpec((N, 4 * QR), lambda g, w: (0, 0)),
            scratch_shapes=[pltpu.VMEM((32 * PIECE, C), F32)],
        ),
        out_shape=jax.ShapeDtypeStruct((N, 4 * QR), F32),
        compiler_params=params(32),
        cost_estimate=pl.CostEstimate(flops=20 * N * N, bytes_accessed=8 * N * N, transcendentals=0),
        name="place",
    )(where, gain, shift, w_own, w_other, *parts)


def gather_z(x):
    def shift(value, by):
        return lax.ppermute(value, "z", [(i, (i + by) % 8) for i in range(8)])

    low, high = shift(x, 1), shift(x, -1)
    far_low = shift(jnp.stack([low, x, high]), 3)
    far_high = shift(jnp.stack([low, x]), -3)
    return jnp.concatenate([far_low, low[None], x[None], high[None], far_high], axis=0)


def attend_kernel(
    where_ref, own_ref, other_ref, query_ref, bias_ref, wk_ref, wv_ref, wq_ref, wg_ref, wo_ref, out_ref
):
    head_of_channel = lax.broadcasted_iota(jnp.int32, (C, 2 * QR), 0) // DH
    second = (lax.broadcasted_iota(jnp.int32, (C, 2 * QR), 1) >= QR).astype(jnp.int32)
    first = lax.broadcasted_iota(jnp.int32, (DH, 2 * QR), 1) < QR
    factor = 1.0 / (ROOT * math.log(2.0))

    def project(m):
        entries = jnp.concatenate([own_ref[m], other_ref[m]], axis=0)
        asked = jnp.concatenate([query_ref[m], query_ref[m]], axis=0)
        keys = jnp.dot(entries, wk_ref[...], preferred_element_type=F32).astype(BF16)
        values = lax.dot_general(wv_ref[...], entries, NT, preferred_element_type=F32).astype(BF16)
        queries = lax.dot_general(wq_ref[...], asked, NT, preferred_element_type=F32)
        gates = jax.nn.sigmoid(lax.dot_general(wg_ref[...], asked, NT, preferred_element_type=F32))
        masked = [jnp.where(head_of_channel == 2 * g + second, queries, 0.0).astype(BF16) for g in range(2)]
        return keys, values, jnp.concatenate(masked, axis=1), gates.astype(BF16).astype(F32)

    projected = [project(m) for m in range(GROUP)]

    def score(m):
        keys, _, masked, _ = projected[m]
        return jnp.dot(keys, masked, preferred_element_type=F32) + bias_ref[...]

    def finish(m, scores):
        _, values, _, gates = projected[m]
        highest = jnp.max(scores, axis=0, keepdims=True)
        exponent = jnp.exp2((scores - highest) * factor)
        totals = jnp.sum(exponent, axis=0, keepdims=True)
        sums = jnp.dot(values, exponent.astype(BF16), preferred_element_type=F32)
        gated = []
        for g in range(2):
            lanes = slice(g * 2 * QR, (g + 1) * 2 * QR)
            low, high = slice(2 * g * DH, (2 * g + 1) * DH), slice((2 * g + 1) * DH, (2 * g + 2) * DH)
            attended = jnp.where(first, sums[low, lanes], sums[high, lanes]) / totals[:, lanes]
            gated.append(attended * jnp.where(first, gates[low], gates[high]))
        turned = jnp.concatenate(gated, axis=0).T.astype(BF16)
        turned = jnp.concatenate([turned[:QR], turned[QR:]], axis=1)
        out_ref[m] = jnp.dot(turned, wo_ref[...], preferred_element_type=F32).astype(BF16)

    scores = score(0)
    for m in range(GROUP):
        following = score(m + 1) if m + 1 < GROUP else None
        finish(m, scores)
        scores = following


def attend(where, own, other, bias, wk, wv, wq, wg, wo):
    weight = pl.BlockSpec((C, C), lambda m, w: (0, 0))
    return pl.pallas_call(
        attend_kernel,
        grid_spec=pltpu.PrefetchScalarGridSpec(
            num_scalar_prefetch=1,
            grid=(COLS // GROUP,),
            in_specs=[
                pl.BlockSpec((GROUP, KH, C), lambda m, w: (m, 0, 0)),
                pl.BlockSpec((GROUP, KH, C), lambda m, w: (m, 0, 0)),
                pl.BlockSpec((GROUP, QR, C), lambda m, w: (m, w[0], 0)),
                pl.BlockSpec((N, 4 * QR), lambda m, w: (0, 0)),
            ]
            + [weight] * 5,
            out_specs=pl.BlockSpec((GROUP, QR, C), lambda m, w: (m, 0, 0)),
        ),
        out_shape=jax.ShapeDtypeStruct((COLS, QR, C), BF16),
        compiler_params=params(48),
        cost_estimate=pl.CostEstimate(
            flops=COLS * 8 * N * N * C, bytes_accessed=12 * N * N, transcendentals=COLS * N * N
        ),
        name="attend",
    )(where, own, other, own, bias, wk, wv, wq, wg, wo)


def local(pair, ln_gain, ln_shift, w_project, w_bias, w_out):
    swap_heads = functools.partial(lax.ppermute, axis_name="h", perm=[(0, 1), (1, 0)])
    swap_cores = functools.partial(lax.ppermute, axis_name="c", perm=[(0, 1), (1, 0)])
    where = [lax.axis_index(name) for name in ("h", "c", "y", "xl", "z")]
    where = jnp.stack(where).astype(jnp.int32)
    gain, shift = ln_gain.reshape(1, C), ln_shift.reshape(1, C)

    rows = normalize(pair, gain, shift)
    blocks = rows.reshape(ROWS, CHIPS, COLS, C).transpose(1, 0, 2, 3).reshape(CHIPS, ROWS * COLS, C)
    arrived = lax.all_to_all(blocks, CHIP, 0, 0, tiled=True)
    own = arrived.reshape(CHIPS, ROWS, COLS, C).transpose(2, 1, 0, 3).reshape(COLS, KH, C)
    other = swap_cores(own)

    weights = jnp.concatenate([w_project.reshape(C, 4 * 64), w_out.T], axis=1)
    weights_other = swap_heads(weights)
    full = [
        jnp.concatenate([weights[:, t * 64 : (t + 1) * 64], weights_other[:, t * 64 : (t + 1) * 64]], axis=1)
        for t in range(5)
    ]
    wo = full[4].T.reshape(2, 2, DH, C).transpose(1, 0, 2, 3).reshape(C, C)
    full = (full[1], full[2].T, full[0].T, full[3].T, wo)

    w_own = jnp.pad(w_bias.T, ((0, 14), (0, 0)))
    w_other = swap_heads(w_own)
    piece = bias_piece(where, pair, swap_cores(pair), gain, shift, w_own, w_other)
    ring = gather_z(piece)
    near = jnp.concatenate([ring, lax.ppermute(ring, "xl", [(0, 1), (1, 0)])], axis=0)
    near, *full = lax.optimization_barrier((near, *full))
    parts = [near] + [lax.ppermute(near, "y", [(i, (i + o) % 4) for i in range(4)]) for o in (1, 2, 3)]
    parts = [part.reshape(32 * PIECE, C) for part in parts]
    bias = place_bias(where, gain, shift, w_own, w_other, parts)

    done = attend(where, own, other, bias, *full)

    sent = done.reshape(COLS, 3, CHIPS, C).transpose(2, 1, 0, 3).reshape(CHIPS, 3 * COLS, C)
    returned = lax.all_to_all(sent, CHIP, 0, 0, tiled=True)
    return returned.reshape(CHIPS, 3, COLS, C).transpose(1, 0, 2, 3).reshape(3, N, C)


def solution(mesh):
    fine = Mesh(mesh.devices.reshape(2, 4, 8, 2, 2), DAP + ("h",))
    in_specs = (P(DAP, None, None), P(), P(), P(None, None, "h"), P(None, "h"), P("h", None))
    out_specs = P(DAP + ("h",), None, None)
    return jax.shard_map(local, mesh=fine, in_specs=in_specs, out_specs=out_specs, check_vma=False)
```

```python
import functools
import math

import jax
import jax.numpy as jnp
from jax import lax
from jax.experimental import pallas as pl
from jax.experimental.pallas import tpu as pltpu
from jax.sharding import Mesh
from jax.sharding import PartitionSpec as P

F32 = jnp.float32
BF16 = jnp.bfloat16
CHIP = ("xl", "y", "z")
DAP = ("xl", "y", "z", "c")
N, C, H, DH = 768, 128, 4, 32
CHIPS, COLS, ROWS = 64, 12, 6
QR = 3 * CHIPS
KH = ROWS * CHIPS
LEVELS = 240
GROUP = 6
SHARE = 18
LAID = 3 * COLS
MESSAGE = 56
ROOT = math.sqrt(DH)
NT = (((1,), (1,)), ((), ()))


def params(mb):
    return pltpu.CompilerParams(vmem_limit_bytes=mb * 2**20)


def layer_norm(x, gain, shift):
    average = jnp.mean(x, axis=-1, keepdims=True)
    centred = x - average
    variance = jnp.mean(centred * centred, axis=-1, keepdims=True)
    return centred * lax.rsqrt(variance + 1e-05) * gain + shift


def bias_range(w, gain, shift):
    w = w.astype(F32)
    middle = jnp.sum(w * shift, axis=1, keepdims=True)
    reach = jnp.sqrt(C * jnp.sum(w * w * gain * gain, axis=1, keepdims=True))
    rounded = jnp.sum(jnp.abs(w * shift), axis=1, keepdims=True)
    return middle, reach * (1 + 1 / 256) + rounded / 256 + 1e-20


def encode(x):
    size = jnp.minimum(jnp.abs(x) * LEVELS, LEVELS - 0.01)
    whole = jnp.floor(size)
    code = jnp.exp2(whole - LEVELS / 2) * (1 + (size - whole))
    return jnp.where(x < 0, -code, code)


def decode(code):
    code = code.astype(F32)
    size = jnp.abs(code)
    whole = jnp.floor(jnp.log2(size))
    x = (whole + (LEVELS / 2 - 1) + size * jnp.exp2(-whole)) / LEVELS
    return jnp.where(code < 0, -x, x)


def lay_kernel(where_ref, own_ref, norm_ref, out_ref, picked_ref, normed, held):
    h = where_ref[0]
    first = 6 * where_ref[1] + 3 * h
    gain, shift = norm_ref[0:1], norm_ref[1:2]
    for r in range(3):
        rows = layer_norm(own_ref[3 * h + r].astype(F32), gain, shift)
        normed[r * N : (r + 1) * N, :] = rows.astype(BF16).astype(F32)
        for q in range(3):
            got = normed[pl.ds(r * N + first + q, CHIPS, stride=COLS), :]
            picked_ref[r, q * CHIPS : (q + 1) * CHIPS, :] = got.astype(BF16)
    for r in range(3):
        held[...] = own_ref[3 * (1 - h) + r].astype(F32)
        got = [held[pl.ds(first + q, CHIPS, stride=COLS), :] for q in range(3)]
        picked_ref[3 + r] = layer_norm(jnp.concatenate(got, axis=0), gain, shift).astype(BF16)
    for p in range(CHIPS):
        for r in range(3):
            to = (p * 3 + r) * COLS
            out_ref[to : to + COLS, :] = normed[r * N + p * COLS : r * N + (p + 1) * COLS, :]


def lay_out(where, pair, norm):
    return pl.pallas_call(
        lay_kernel,
        grid_spec=pltpu.PrefetchScalarGridSpec(
            num_scalar_prefetch=1,
            grid=(1,),
            in_specs=[
                pl.BlockSpec((ROWS, N, C), lambda g, w: (0, 0, 0)),
                pl.BlockSpec((2, C), lambda g, w: (0, 0)),
            ],
            out_specs=[
                pl.BlockSpec((3 * N, C), lambda g, w: (0, 0)),
                pl.BlockSpec((ROWS, QR, C), lambda g, w: (0, 0, 0)),
            ],
            scratch_shapes=[pltpu.VMEM((3 * N, C), F32), pltpu.VMEM((N, C), F32)],
        ),
        out_shape=[
            jax.ShapeDtypeStruct((3 * N, C), F32),
            jax.ShapeDtypeStruct((ROWS, QR, C), BF16),
        ],
        compiler_params=params(24),
        cost_estimate=pl.CostEstimate(flops=20 * N * ROWS * C, bytes_accessed=6 * ROWS * N * C, transcendentals=0),
        name="lay",
    )(where, pair, norm)


def pack_kernel(
    where_ref, laid_ref, picked_ref, other_ref, norm_ref, w_own_ref, w_other_ref, out_ref, held, coded, tail
):
    h = where_ref[0]
    first = 6 * where_ref[1] + 3 * h
    gain, shift = norm_ref[0:1], norm_ref[1:2]
    weights = [w_ref[...] for w_ref in (w_own_ref, w_other_ref)]
    ranges = [bias_range(w, gain, shift) for w in weights]

    def code_row(at, entries):
        parts = [
            (lax.dot_general(w, entries, NT, preferred_element_type=F32) - middle) / reach
            for w, (middle, reach) in zip(weights, ranges)
        ]
        row = jnp.concatenate([part[g : g + 1] for part in parts for g in range(2)], axis=1)
        for s in range(6):
            coded[at * 6 + s : at * 6 + s + 1, :] = row[:, s * C : (s + 1) * C]

    for half in range(2):
        for r in range(3):
            code_row(half * 6 + r, picked_ref[half * 3 + r])
            held[...] = other_ref[3 * (h if half == 0 else 1 - h) + r].astype(F32)
            got = [held[pl.ds(first + q, CHIPS, stride=COLS), :] for q in range(3)]
            entries = layer_norm(jnp.concatenate(got, axis=0), gain, shift).astype(BF16)
            code_row(half * 6 + 3 + r, entries)
    coded[...] = encode(coded[...])
    for p in range(CHIPS):
        y = p // 8 % 4
        tail[p * 24 : p * 24 + 4, :] = laid_ref[p * LAID + 32 : (p + 1) * LAID, :]
        tail[p * 24 + 4 : p * 24 + 4 + SHARE, :] = coded[y * SHARE : (y + 1) * SHARE, :]
        tail[p * 24 + 4 + SHARE : (p + 1) * 24, :] = jnp.zeros((20 - SHARE, C), F32)
    for p in range(CHIPS):
        out_ref[p, :32, :] = laid_ref[p * LAID : p * LAID + 32, :].astype(BF16)
        out_ref[p, 32:, :] = tail[p * 24 : (p + 1) * 24, :].astype(BF16)


def pack(where, laid, picked, other, norm, w_own, w_other):
    return pl.pallas_call(
        pack_kernel,
        grid_spec=pltpu.PrefetchScalarGridSpec(
            num_scalar_prefetch=1,
            grid=(1,),
            in_specs=[
                pl.BlockSpec((3 * N, C), lambda g, w: (0, 0)),
                pl.BlockSpec((ROWS, QR, C), lambda g, w: (0, 0, 0)),
                pl.BlockSpec((ROWS, N, C), lambda g, w: (0, 0, 0)),
                pl.BlockSpec((2, C), lambda g, w: (0, 0)),
                pl.BlockSpec((16, C), lambda g, w: (0, 0)),
                pl.BlockSpec((16, C), lambda g, w: (0, 0)),
            ],
            out_specs=pl.BlockSpec((CHIPS, MESSAGE, C), lambda g, w: (0, 0, 0)),
            scratch_shapes=[
                pltpu.VMEM((N, C), F32),
                pltpu.VMEM((4 * SHARE, C), F32),
                pltpu.VMEM((CHIPS * 24, C), F32),
            ],
        ),
        out_shape=jax.ShapeDtypeStruct((CHIPS, MESSAGE, C), BF16),
        compiler_params=params(24),
        cost_estimate=pl.CostEstimate(flops=60 * N * ROWS * C, bytes_accessed=6 * ROWS * N * C, transcendentals=0),
        name="pack",
    )(where, laid, picked, other, norm, w_own, w_other)


def unpack_kernel(arrived_ref, share_ref, column_ref, held):
    held[...] = arrived_ref[...].astype(F32).reshape(CHIPS * MESSAGE, C)
    for j in range(SHARE):
        got = held[pl.ds(LAID + j, CHIPS, stride=MESSAGE), :]
        share_ref[j * CHIPS : (j + 1) * CHIPS, :] = got.astype(BF16)
    for m in range(COLS):
        for r in range(3):
            got = held[pl.ds(r * COLS + m, CHIPS, stride=MESSAGE), :]
            column_ref[m, r * CHIPS : (r + 1) * CHIPS, :] = got.astype(BF16)


def unpack(arrived):
    return pl.pallas_call(
        unpack_kernel,
        out_shape=[
            jax.ShapeDtypeStruct((SHARE * CHIPS, C), BF16),
            jax.ShapeDtypeStruct((COLS, QR, C), BF16),
        ],
        scratch_shapes=[pltpu.VMEM((CHIPS * MESSAGE, C), F32)],
        compiler_params=params(24),
        cost_estimate=pl.CostEstimate(flops=CHIPS * MESSAGE * C, bytes_accessed=8 * CHIPS * MESSAGE * C, transcendentals=0),
        name="unpack",
    )(arrived)


def place_kernel(where_ref, norm_ref, w_own_ref, w_other_ref, part_ref, *refs):
    out_ref = refs[-1]
    reaches = [bias_range(w_ref[...], norm_ref[0:1], norm_ref[1:2])[1] for w_ref in (w_own_ref, w_other_ref)]
    scale = [jnp.broadcast_to(reach[g : g + 1] * ROOT, (8, QR)) for reach in reaches for g in range(2)]
    scale = jnp.concatenate(scale, axis=1)[:1]
    for a in range(3):
        for s in range(6):
            lanes = slice(s * C, (s + 1) * C)
            at = (a * 6 + s) * CHIPS
            out_ref[a * CHIPS : (a + 1) * CHIPS, lanes] = decode(part_ref[at : at + CHIPS, :]) * scale[:, lanes]


def place_bias(where, norm, w_own, w_other, part, step, bias):
    small = lambda g, w: (0, 0)
    in_specs = [
        pl.BlockSpec((2, C), small),
        pl.BlockSpec((16, C), small),
        pl.BlockSpec((16, C), small),
        pl.BlockSpec((SHARE * CHIPS, C), small),
    ]
    operands = [where, norm, w_own, w_other, part]
    aliases = {}
    if bias is not None:
        in_specs.append(pl.BlockSpec(memory_space=pl.ANY))
        operands.append(bias)
        aliases = {5: 0}
    return pl.pallas_call(
        place_kernel,
        grid_spec=pltpu.PrefetchScalarGridSpec(
            num_scalar_prefetch=1,
            grid=(1,),
            in_specs=in_specs,
            out_specs=pl.BlockSpec((QR, 4 * QR), lambda g, w: (lax.rem(w[2] - step + 4, 4), 0)),
        ),
        out_shape=jax.ShapeDtypeStruct((N, 4 * QR), F32),
        input_output_aliases=aliases,
        compiler_params=params(16),
        cost_estimate=pl.CostEstimate(flops=5 * N * N, bytes_accessed=2 * N * N, transcendentals=0),
        name="place",
    )(*operands)


def project_kernel(own_ref, other_ref, wk_ref, wv_ref, keys_ref, values_ref):
    for m in range(GROUP):
        entries = jnp.concatenate([own_ref[m], other_ref[m]], axis=0)
        keys_ref[m] = jnp.dot(entries, wk_ref[...], preferred_element_type=F32).astype(BF16)
        values_ref[m] = lax.dot_general(wv_ref[...], entries, NT, preferred_element_type=F32).astype(BF16)


def project(own, other, wk, wv):
    block = pl.BlockSpec((GROUP, QR, C), lambda m: (m, 0, 0))
    weight = pl.BlockSpec((C, C), lambda m: (0, 0))
    shapes = [(2 * QR, C), (C, 2 * QR)]
    return pl.pallas_call(
        project_kernel,
        grid=(COLS // GROUP,),
        in_specs=[block, block, weight, weight],
        out_specs=[pl.BlockSpec((GROUP,) + shape, lambda m: (m, 0, 0)) for shape in shapes],
        out_shape=[jax.ShapeDtypeStruct((COLS,) + shape, BF16) for shape in shapes],
        compiler_params=params(16),
        cost_estimate=pl.CostEstimate(flops=COLS * 2 * N * C * C, bytes_accessed=10 * N * N, transcendentals=0),
        name="project",
    )(own, other, wk, wv)


def ask_kernel(own_ref, wq_ref, wg_ref, masked_ref, gates_ref):
    head_of_channel = lax.broadcasted_iota(jnp.int32, (C, 2 * QR), 0) // DH
    second = (lax.broadcasted_iota(jnp.int32, (C, 2 * QR), 1) >= QR).astype(jnp.int32)
    first = lax.broadcasted_iota(jnp.int32, (DH, 2 * QR), 1) < QR
    for m in range(GROUP):
        asked = jnp.concatenate([own_ref[m], own_ref[m]], axis=0)
        queries = lax.dot_general(wq_ref[...], asked, NT, preferred_element_type=F32)
        gates = jax.nn.sigmoid(lax.dot_general(wg_ref[...], asked, NT, preferred_element_type=F32))
        for g in range(2):
            lanes = slice(g * 2 * QR, (g + 1) * 2 * QR)
            low, high = slice(2 * g * DH, (2 * g + 1) * DH), slice((2 * g + 1) * DH, (2 * g + 2) * DH)
            masked_ref[m, :, lanes] = jnp.where(head_of_channel == 2 * g + second, queries, 0.0).astype(BF16)
            gates_ref[m, g * DH : (g + 1) * DH, :] = jnp.where(first, gates[low], gates[high]).astype(BF16)


def ask(own, wq, wg):
    weight = pl.BlockSpec((C, C), lambda m: (0, 0))
    shapes = [(C, 4 * QR), (2 * DH, 2 * QR)]
    return pl.pallas_call(
        ask_kernel,
        grid=(COLS // GROUP,),
        in_specs=[pl.BlockSpec((GROUP, QR, C), lambda m: (m, 0, 0)), weight, weight],
        out_specs=[pl.BlockSpec((GROUP,) + shape, lambda m: (m, 0, 0)) for shape in shapes],
        out_shape=[jax.ShapeDtypeStruct((COLS,) + shape, BF16) for shape in shapes],
        compiler_params=params(16),
        cost_estimate=pl.CostEstimate(flops=COLS * 2 * N * C * C, bytes_accessed=10 * N * N, transcendentals=0),
        name="ask",
    )(own, wq, wg)


def attend_kernel(k0_ref, v0_ref, k1_ref, v1_ref, masked_ref, gates_ref, bias_ref, wo_ref, out_ref):
    first = lax.broadcasted_iota(jnp.int32, (DH, 2 * QR), 1) < QR
    factor = 1.0 / (ROOT * math.log(2.0))

    def score(m):
        keys = jnp.concatenate([k0_ref[m], k1_ref[m]], axis=0)
        return jnp.dot(keys, masked_ref[m], preferred_element_type=F32) + bias_ref[...]

    def soften(m, scores):
        highest = jnp.max(scores, axis=0, keepdims=True)
        exponent = jnp.exp2((scores - highest) * factor)
        totals = jnp.sum(exponent, axis=0, keepdims=True)
        values = jnp.concatenate([v0_ref[m], v1_ref[m]], axis=1)
        return jnp.dot(values, exponent.astype(BF16), preferred_element_type=F32), totals

    def finish(m, sums, totals):
        gated = []
        for g in range(2):
            lanes = slice(g * 2 * QR, (g + 1) * 2 * QR)
            low, high = slice(2 * g * DH, (2 * g + 1) * DH), slice((2 * g + 1) * DH, (2 * g + 2) * DH)
            attended = jnp.where(first, sums[low, lanes], sums[high, lanes]) / totals[:, lanes]
            gated.append(attended * gates_ref[m, g * DH : (g + 1) * DH, :].astype(F32))
        turned = jnp.concatenate(gated, axis=0).T.astype(BF16)
        turned = jnp.concatenate([turned[:QR], turned[QR:]], axis=1)
        out_ref[m] = jnp.dot(turned, wo_ref[...], preferred_element_type=F32).astype(BF16)

    attended = []
    scores = score(0)
    for m in range(GROUP):
        following = score(m + 1) if m + 1 < GROUP else None
        attended.append(soften(m, scores))
        scores = following
    for m in range(GROUP):
        finish(m, *attended[m])


def attend(k0, v0, k1, v1, masked, gates, bias, wo):
    shapes = [(2 * QR, C), (C, 2 * QR)] * 2 + [(C, 4 * QR), (2 * DH, 2 * QR)]
    return pl.pallas_call(
        attend_kernel,
        grid=(COLS // GROUP,),
        in_specs=[pl.BlockSpec((GROUP,) + shape, lambda m: (m, 0, 0)) for shape in shapes]
        + [pl.BlockSpec((N, 4 * QR), lambda m: (0, 0)), pl.BlockSpec((C, C), lambda m: (0, 0))],
        out_specs=pl.BlockSpec((GROUP, QR, C), lambda m: (m, 0, 0)),
        out_shape=jax.ShapeDtypeStruct((COLS, QR, C), BF16),
        compiler_params=params(40),
        cost_estimate=pl.CostEstimate(
            flops=COLS * 8 * N * N * C, bytes_accessed=12 * N * N, transcendentals=COLS * N * N
        ),
        name="attend",
    )(k0, v0, k1, v1, masked, gates, bias, wo)


def local(pair, ln_gain, ln_shift, w_project, w_bias, w_out):
    swap_heads = functools.partial(lax.ppermute, axis_name="h", perm=[(0, 1), (1, 0)])
    swap_cores = functools.partial(lax.ppermute, axis_name="c", perm=[(0, 1), (1, 0)])
    where = [lax.axis_index(name) for name in ("h", "c", "y", "xl", "z")]
    where = jnp.stack(where).astype(jnp.int32)
    norm = jnp.stack([ln_gain, ln_shift])

    w_own = jnp.pad(w_bias.T, ((0, 14), (0, 0)))
    w_other = swap_heads(w_own)
    laid, picked = lay_out(where, pair, norm)
    blocks = pack(where, laid, picked, swap_cores(pair), norm, w_own, w_other)
    arrived = lax.all_to_all(blocks, CHIP, 0, 0, tiled=True)
    weights = jnp.concatenate([w_project.reshape(C, 4 * 64), w_out.T], axis=1)
    weights_other = swap_heads(weights)
    full = [
        jnp.concatenate([weights[:, t * 64 : (t + 1) * 64], weights_other[:, t * 64 : (t + 1) * 64]], axis=1)
        for t in range(5)
    ]
    wo = full[4].T.reshape(2, 2, DH, C).transpose(1, 0, 2, 3).reshape(C, C)
    full = (full[1], full[2].T, full[0].T, full[3].T, wo)
    arrived, *full = lax.optimization_barrier((arrived, *full))

    wk, wv, wq, wg, wo = full
    share, own = unpack(arrived)
    far = swap_heads(own)
    parts = [share] + [lax.ppermute(share, "y", [(i, (i + o) % 4) for i in range(4)]) for o in (1, 2, 3)]
    masked, gates = ask(own, wq, wg)
    k0, v0 = project(own, swap_cores(own), wk, wv)
    bias = place_bias(where, norm, w_own, w_other, share, 0, None)
    waited = (far, *parts, masked, gates, k0, v0, bias)
    far, *parts, masked, gates, k0, v0, bias = lax.optimization_barrier(waited)
    k1, v1 = project(far, swap_cores(far), wk, wv)
    for step in (3, 2, 1):
        bias = place_bias(where, norm, w_own, w_other, parts[step], step, bias)
    done = attend(k0, v0, k1, v1, masked, gates, bias, wo)

    sent = done.reshape(COLS, 3, CHIPS, C).transpose(2, 1, 0, 3).reshape(CHIPS, 3 * COLS, C)
    returned = lax.all_to_all(sent, CHIP, 0, 0, tiled=True)
    return returned.reshape(CHIPS, 3, COLS, C).transpose(1, 0, 2, 3).reshape(3, N, C)


def solution(mesh):
    fine = Mesh(mesh.devices.reshape(2, 4, 8, 2, 2), DAP + ("h",))
    in_specs = (P(DAP, None, None), P(), P(), P(None, None, "h"), P(None, "h"), P("h", None))
    out_specs = P(DAP + ("h",), None, None)
    return jax.shard_map(local, mesh=fine, in_specs=in_specs, out_specs=out_specs, check_vma=False)
```

```python
import functools
import math

import jax
import jax.numpy as jnp
from jax import lax
from jax.experimental import pallas as pl
from jax.experimental.pallas import tpu as pltpu
from jax.sharding import Mesh
from jax.sharding import PartitionSpec as P

F32 = jnp.float32
BF16 = jnp.bfloat16
CHIP = ("xl", "y", "z")
DAP = ("xl", "y", "z", "c")
N, C, H, DH = 768, 128, 4, 32
CHIPS, COLS, ROWS = 64, 12, 6
QR = 3 * CHIPS
KH = ROWS * CHIPS
LEVELS = 240
GROUP = 6
SHARE = 18
LAID = 3 * COLS
MESSAGE = 56
ROOT = math.sqrt(DH)
NT = (((1,), (1,)), ((), ()))
VMEM = pl.BlockSpec(memory_space=pltpu.VMEM)
SMEM = pl.BlockSpec(memory_space=pltpu.SMEM)


def params(mb):
    return pltpu.CompilerParams(vmem_limit_bytes=mb * 2**20)


def layer_norm(x, gain, shift):
    average = jnp.mean(x, axis=-1, keepdims=True)
    centred = x - average
    variance = jnp.mean(centred * centred, axis=-1, keepdims=True)
    return centred * lax.rsqrt(variance + 1e-05) * gain + shift


def bias_range(w, gain, shift):
    w = w.astype(F32)
    middle = jnp.sum(w * shift, axis=1, keepdims=True)
    reach = jnp.sqrt(C * jnp.sum(w * w * gain * gain, axis=1, keepdims=True))
    rounded = jnp.sum(jnp.abs(w * shift), axis=1, keepdims=True)
    return middle, reach * (1 + 1 / 256) + rounded / 256 + 1e-20


def head_weights(own_ref, other_ref):
    own, other = own_ref[...].astype(F32), other_ref[...].astype(F32)
    return jnp.concatenate([own[:2], other[:2], own[4:16]], axis=0)


def encode(x):
    size = jnp.minimum(jnp.abs(x) * LEVELS, LEVELS - 0.01)
    whole = jnp.floor(size)
    code = jnp.exp2(whole - LEVELS / 2) * (1 + (size - whole))
    return jnp.where(x < 0, -code, code)


def decode(code):
    code = code.astype(F32)
    size = jnp.abs(code)
    whole = jnp.floor(jnp.log2(size))
    x = (whole + (LEVELS / 2 - 1) + size * jnp.exp2(-whole)) / LEVELS
    return jnp.where(code < 0, -x, x)


def lay_kernel(where_ref, own_ref, norm_ref, out_ref, picked_ref, normed, held):
    h = where_ref[0]
    first = 6 * where_ref[1] + 3 * h
    gain, shift = norm_ref[0:1], norm_ref[1:2]
    for r in range(3):
        rows = layer_norm(own_ref[3 * h + r].astype(F32), gain, shift)
        normed[r * N : (r + 1) * N, :] = rows.astype(BF16).astype(F32)
        for q in range(3):
            got = normed[pl.ds(r * N + first + q, CHIPS, stride=COLS), :]
            at = r * QR + q * CHIPS
            picked_ref[at : at + CHIPS, :] = got.astype(BF16)
    for r in range(3):
        held[...] = own_ref[3 * (1 - h) + r].astype(F32)
        got = [held[pl.ds(first + q, CHIPS, stride=COLS), :] for q in range(3)]
        at = (3 + r) * QR
        picked_ref[at : at + QR, :] = layer_norm(jnp.concatenate(got, axis=0), gain, shift).astype(BF16)
    for p in range(CHIPS):
        for r in range(3):
            to = (p * 3 + r) * COLS
            out_ref[to : to + COLS, :] = normed[r * N + p * COLS : r * N + (p + 1) * COLS, :]


def lay_out(where, pair, norm):
    return pl.pallas_call(
        lay_kernel,
        in_specs=[SMEM, VMEM, VMEM],
        out_specs=[VMEM, VMEM],
        scratch_shapes=[pltpu.VMEM((3 * N, C), F32), pltpu.VMEM((N, C), F32)],
        out_shape=[
            jax.ShapeDtypeStruct((3 * N, C), F32),
            jax.ShapeDtypeStruct((ROWS * QR, C), BF16),
        ],
        compiler_params=params(24),
        cost_estimate=pl.CostEstimate(flops=20 * N * ROWS * C, bytes_accessed=6 * ROWS * N * C, transcendentals=0),
        name="lay",
    )(where, pair, norm)


def pack_kernel(
    where_ref, laid_ref, picked_ref, other_ref, norm_ref, w_own_ref, w_other_ref, out_ref, held, coded, tail
):
    h = where_ref[0]
    first = 6 * where_ref[1] + 3 * h
    gain, shift = norm_ref[0:1], norm_ref[1:2]
    weights = head_weights(w_own_ref, w_other_ref)
    middle, reach = bias_range(weights, gain, shift)
    entries = []
    for half in range(2):
        entries.append(picked_ref[half * 3 * QR : (half + 1) * 3 * QR, :])
        for r in range(3):
            held[...] = other_ref[3 * (h if half == 0 else 1 - h) + r].astype(F32)
            got = [held[pl.ds(first + q, CHIPS, stride=COLS), :] for q in range(3)]
            entries.append(layer_norm(jnp.concatenate(got, axis=0), gain, shift).astype(BF16))
    entries = jnp.concatenate(entries, axis=0)
    bias = lax.dot_general(weights.astype(BF16), entries, NT, preferred_element_type=F32)
    codes = encode((bias - middle) / reach)
    for at in range(2 * ROWS):
        row = [codes[g : g + 1, at * QR : (at + 1) * QR] for g in range(H)]
        row = jnp.concatenate(row, axis=1)
        for s in range(6):
            coded[at * 6 + s : at * 6 + s + 1, :] = row[:, s * C : (s + 1) * C]
    for p in range(CHIPS):
        y = p // 8 % 4
        tail[p * 24 : p * 24 + 4, :] = laid_ref[p * LAID + 32 : (p + 1) * LAID, :]
        tail[p * 24 + 4 : p * 24 + 4 + SHARE, :] = coded[y * SHARE : (y + 1) * SHARE, :]
        tail[p * 24 + 4 + SHARE : (p + 1) * 24, :] = jnp.zeros((20 - SHARE, C), F32)
    for p in range(CHIPS):
        out_ref[p, :32, :] = laid_ref[p * LAID : p * LAID + 32, :].astype(BF16)
        out_ref[p, 32:, :] = tail[p * 24 : (p + 1) * 24, :].astype(BF16)


def pack(where, laid, picked, other, norm, w_own, w_other):
    return pl.pallas_call(
        pack_kernel,
        in_specs=[SMEM] + [VMEM] * 6,
        out_specs=VMEM,
        scratch_shapes=[
            pltpu.VMEM((N, C), F32),
            pltpu.VMEM((4 * SHARE, C), F32),
            pltpu.VMEM((CHIPS * 24, C), F32),
        ],
        out_shape=jax.ShapeDtypeStruct((CHIPS, MESSAGE, C), BF16),
        compiler_params=params(24),
        cost_estimate=pl.CostEstimate(flops=60 * N * ROWS * C, bytes_accessed=6 * ROWS * N * C, transcendentals=0),
        name="pack",
    )(where, laid, picked, other, norm, w_own, w_other)


def unpack_kernel(arrived_ref, share_ref, column_ref, held):
    held[...] = arrived_ref[...].astype(F32).reshape(CHIPS * MESSAGE, C)
    for j in range(SHARE):
        got = held[pl.ds(LAID + j, CHIPS, stride=MESSAGE), :]
        share_ref[j * CHIPS : (j + 1) * CHIPS, :] = got.astype(BF16)
    for m in range(COLS):
        for r in range(3):
            got = held[pl.ds(r * COLS + m, CHIPS, stride=MESSAGE), :]
            column_ref[m, r * CHIPS : (r + 1) * CHIPS, :] = got.astype(BF16)


def unpack(arrived):
    return pl.pallas_call(
        unpack_kernel,
        out_shape=[
            jax.ShapeDtypeStruct((SHARE * CHIPS, C), BF16),
            jax.ShapeDtypeStruct((COLS, QR, C), BF16),
        ],
        scratch_shapes=[pltpu.VMEM((CHIPS * MESSAGE, C), F32)],
        compiler_params=params(24),
        cost_estimate=pl.CostEstimate(flops=CHIPS * MESSAGE * C, bytes_accessed=8 * CHIPS * MESSAGE * C, transcendentals=0),
        name="unpack",
    )(arrived)


def place_kernel(where_ref, norm_ref, w_own_ref, w_other_ref, part_ref, *refs):
    out_ref = refs[-1]
    reaches = [bias_range(w_ref[...], norm_ref[0:1], norm_ref[1:2])[1] for w_ref in (w_own_ref, w_other_ref)]
    scale = [jnp.broadcast_to(reach[g : g + 1] * ROOT, (8, QR)) for reach in reaches for g in range(2)]
    scale = jnp.concatenate(scale, axis=1)[:1]
    for a in range(3):
        for s in range(6):
            lanes = slice(s * C, (s + 1) * C)
            at = (a * 6 + s) * CHIPS
            out_ref[a * CHIPS : (a + 1) * CHIPS, lanes] = decode(part_ref[at : at + CHIPS, :]) * scale[:, lanes]


def place_bias(where, norm, w_own, w_other, part, step, bias):
    small = lambda g, w: (0, 0)
    in_specs = [
        pl.BlockSpec((2, C), small),
        pl.BlockSpec((16, C), small),
        pl.BlockSpec((16, C), small),
        pl.BlockSpec((SHARE * CHIPS, C), small),
    ]
    operands = [where, norm, w_own, w_other, part]
    aliases = {}
    if bias is not None:
        in_specs.append(pl.BlockSpec(memory_space=pl.ANY))
        operands.append(bias)
        aliases = {5: 0}
    return pl.pallas_call(
        place_kernel,
        grid_spec=pltpu.PrefetchScalarGridSpec(
            num_scalar_prefetch=1,
            grid=(1,),
            in_specs=in_specs,
            out_specs=pl.BlockSpec((QR, 4 * QR), lambda g, w: (lax.rem(w[2] - step + 4, 4), 0)),
        ),
        out_shape=jax.ShapeDtypeStruct((N, 4 * QR), F32),
        input_output_aliases=aliases,
        compiler_params=params(16),
        cost_estimate=pl.CostEstimate(flops=5 * N * N, bytes_accessed=2 * N * N, transcendentals=0),
        name="place",
    )(*operands)


def project_kernel(own_ref, other_ref, wk_ref, wv_ref, keys_ref, values_ref):
    for m in range(GROUP):
        entries = jnp.concatenate([own_ref[m], other_ref[m]], axis=0)
        keys_ref[m] = jnp.dot(entries, wk_ref[...], preferred_element_type=F32).astype(BF16)
        values_ref[m] = lax.dot_general(wv_ref[...], entries, NT, preferred_element_type=F32).astype(BF16)


def project(own, other, wk, wv):
    block = pl.BlockSpec((GROUP, QR, C), lambda m: (m, 0, 0))
    weight = pl.BlockSpec((C, C), lambda m: (0, 0))
    shapes = [(2 * QR, C), (C, 2 * QR)]
    return pl.pallas_call(
        project_kernel,
        grid=(COLS // GROUP,),
        in_specs=[block, block, weight, weight],
        out_specs=[pl.BlockSpec((GROUP,) + shape, lambda m: (m, 0, 0)) for shape in shapes],
        out_shape=[jax.ShapeDtypeStruct((COLS,) + shape, BF16) for shape in shapes],
        compiler_params=params(16),
        cost_estimate=pl.CostEstimate(flops=COLS * 2 * N * C * C, bytes_accessed=10 * N * N, transcendentals=0),
        name="project",
    )(own, other, wk, wv)


def ask_kernel(own_ref, wq_ref, wg_ref, masked_ref, gates_ref):
    head_of_channel = lax.broadcasted_iota(jnp.int32, (C, 2 * QR), 0) // DH
    second = (lax.broadcasted_iota(jnp.int32, (C, 2 * QR), 1) >= QR).astype(jnp.int32)
    first = lax.broadcasted_iota(jnp.int32, (DH, 2 * QR), 1) < QR
    for m in range(GROUP):
        asked = jnp.concatenate([own_ref[m], own_ref[m]], axis=0)
        queries = lax.dot_general(wq_ref[...], asked, NT, preferred_element_type=F32)
        gates = jax.nn.sigmoid(lax.dot_general(wg_ref[...], asked, NT, preferred_element_type=F32))
        for g in range(2):
            lanes = slice(g * 2 * QR, (g + 1) * 2 * QR)
            low, high = slice(2 * g * DH, (2 * g + 1) * DH), slice((2 * g + 1) * DH, (2 * g + 2) * DH)
            masked_ref[m, :, lanes] = jnp.where(head_of_channel == 2 * g + second, queries, 0.0).astype(BF16)
            gates_ref[m, g * DH : (g + 1) * DH, :] = jnp.where(first, gates[low], gates[high]).astype(BF16)


def ask(own, wq, wg):
    weight = pl.BlockSpec((C, C), lambda m: (0, 0))
    shapes = [(C, 4 * QR), (2 * DH, 2 * QR)]
    return pl.pallas_call(
        ask_kernel,
        grid=(COLS // GROUP,),
        in_specs=[pl.BlockSpec((GROUP, QR, C), lambda m: (m, 0, 0)), weight, weight],
        out_specs=[pl.BlockSpec((GROUP,) + shape, lambda m: (m, 0, 0)) for shape in shapes],
        out_shape=[jax.ShapeDtypeStruct((COLS,) + shape, BF16) for shape in shapes],
        compiler_params=params(16),
        cost_estimate=pl.CostEstimate(flops=COLS * 2 * N * C * C, bytes_accessed=10 * N * N, transcendentals=0),
        name="ask",
    )(own, wq, wg)


def attend_kernel(k0_ref, v0_ref, k1_ref, v1_ref, masked_ref, gates_ref, bias_ref, wo_ref, out_ref):
    first = lax.broadcasted_iota(jnp.int32, (DH, 2 * QR), 1) < QR
    factor = 1.0 / (ROOT * math.log(2.0))

    def score(m):
        keys = jnp.concatenate([k0_ref[m], k1_ref[m]], axis=0)
        return jnp.dot(keys, masked_ref[m], preferred_element_type=F32) + bias_ref[...]

    def soften(m, scores):
        highest = jnp.max(scores, axis=0, keepdims=True)
        exponent = jnp.exp2((scores - highest) * factor)
        totals = jnp.sum(exponent, axis=0, keepdims=True)
        weights = exponent.astype(BF16)
        values = jnp.concatenate([v0_ref[m], v1_ref[m]], axis=1)
        low = jnp.dot(values[: 2 * DH], weights[:, :256], preferred_element_type=F32)
        both = jnp.dot(values, weights[:, 256:512], preferred_element_type=F32)
        high = jnp.dot(values[2 * DH :], weights[:, 512:], preferred_element_type=F32)
        low = jnp.concatenate([low, both[: 2 * DH, :128]], axis=1)
        high = jnp.concatenate([both[2 * DH :, 128:], high], axis=1)
        return (low, high), totals

    def finish(m, sums, totals):
        gated = []
        for g in range(2):
            lanes = slice(g * 2 * QR, (g + 1) * 2 * QR)
            attended = jnp.where(first, sums[g][:DH], sums[g][DH:]) / totals[:, lanes]
            gated.append(attended * gates_ref[m, g * DH : (g + 1) * DH, :].astype(F32))
        turned = jnp.concatenate(gated, axis=0).T.astype(BF16)
        turned = jnp.concatenate([turned[:QR], turned[QR:]], axis=1)
        out_ref[m] = jnp.dot(turned, wo_ref[...], preferred_element_type=F32).astype(BF16)

    attended = []
    scores = score(0)
    for m in range(COLS):
        following = score(m + 1) if m + 1 < COLS else None
        attended.append(soften(m, scores))
        scores = following
    for m in range(COLS):
        finish(m, *attended[m])


def attend(k0, v0, k1, v1, masked, gates, bias, wo):
    return pl.pallas_call(
        attend_kernel,
        in_specs=[VMEM] * 8,
        out_specs=VMEM,
        out_shape=jax.ShapeDtypeStruct((COLS, QR, C), BF16),
        compiler_params=params(40),
        cost_estimate=pl.CostEstimate(
            flops=COLS * 8 * N * N * C, bytes_accessed=12 * N * N, transcendentals=COLS * N * N
        ),
        name="attend",
    )(k0, v0, k1, v1, masked, gates, bias, wo)


def local(pair, ln_gain, ln_shift, w_project, w_bias, w_out):
    swap_heads = functools.partial(lax.ppermute, axis_name="h", perm=[(0, 1), (1, 0)])
    swap_cores = functools.partial(lax.ppermute, axis_name="c", perm=[(0, 1), (1, 0)])
    where = [lax.axis_index(name) for name in ("h", "c", "y", "xl", "z")]
    where = jnp.stack(where).astype(jnp.int32)
    norm = jnp.stack([ln_gain, ln_shift])

    w_own = jnp.pad(w_bias.T, ((0, 14), (0, 0)))
    w_other = swap_heads(w_own)
    laid, picked = lay_out(where, pair, norm)
    blocks = pack(where, laid, picked, swap_cores(pair), norm, w_own, w_other)
    arrived = lax.all_to_all(blocks, CHIP, 0, 0, tiled=True)
    weights = jnp.concatenate([w_project.reshape(C, 4 * 64), w_out.T], axis=1)
    weights_other = swap_heads(weights)
    full = [
        jnp.concatenate([weights[:, t * 64 : (t + 1) * 64], weights_other[:, t * 64 : (t + 1) * 64]], axis=1)
        for t in range(5)
    ]
    wo = full[4].T.reshape(2, 2, DH, C).transpose(1, 0, 2, 3).reshape(C, C)
    full = (full[1], full[2].T, full[0].T, full[3].T, wo)
    arrived, *full = lax.optimization_barrier((arrived, *full))

    wk, wv, wq, wg, wo = full
    share, own = unpack(arrived)
    far = swap_heads(own)
    parts = [share] + [lax.ppermute(share, "y", [(i, (i + o) % 4) for i in range(4)]) for o in (1, 2, 3)]
    masked, gates = ask(own, wq, wg)
    k0, v0 = project(own, swap_cores(own), wk, wv)
    bias = place_bias(where, norm, w_own, w_other, share, 0, None)
    waited = (parts[3], masked, gates, k0, v0, bias)
    parts[3], masked, gates, k0, v0, bias = lax.optimization_barrier(waited)
    for step in (3, 2):
        bias = place_bias(where, norm, w_own, w_other, parts[step], step, bias)
    far, parts[1], bias = lax.optimization_barrier((far, parts[1], bias))
    k1, v1 = project(far, swap_cores(far), wk, wv)
    bias = place_bias(where, norm, w_own, w_other, parts[1], 1, bias)
    done = attend(k0, v0, k1, v1, masked, gates, bias, wo)

    sent = done.reshape(COLS, 3, CHIPS, C).transpose(2, 1, 0, 3).reshape(CHIPS, 9, 4, C)
    returned = lax.all_to_all(sent, CHIP, 0, 0, tiled=True)
    return returned.reshape(CHIPS, 3, COLS, C).transpose(1, 0, 2, 3).reshape(3, N, C)


def solution(mesh):
    fine = Mesh(mesh.devices.reshape(2, 4, 8, 2, 2), DAP + ("h",))
    in_specs = (P(DAP, None, None), P(), P(), P(None, None, "h"), P(None, "h"), P("h", None))
    out_specs = P(DAP + ("h",), None, None)
    return jax.shard_map(local, mesh=fine, in_specs=in_specs, out_specs=out_specs, check_vma=False)
```

```python
import functools
import math

import jax
import jax.numpy as jnp
from jax import lax
from jax.experimental import pallas as pl
from jax.experimental.pallas import tpu as pltpu
from jax.sharding import Mesh
from jax.sharding import PartitionSpec as P

F32 = jnp.float32
BF16 = jnp.bfloat16
CHIP = ("xl", "y", "z")
DAP = ("xl", "y", "z", "c")
N, C, H, DH = 768, 128, 4, 32
CHIPS, COLS, ROWS = 64, 12, 6
QR = 3 * CHIPS
KH = ROWS * CHIPS
LEVELS = 240
GROUP = 6
SHARE = 18
LAID = 3 * COLS
MESSAGE = 56
ROOT = math.sqrt(DH)
NT = (((1,), (1,)), ((), ()))
VMEM = pl.BlockSpec(memory_space=pltpu.VMEM)
SMEM = pl.BlockSpec(memory_space=pltpu.SMEM)


def params(mb):
    return pltpu.CompilerParams(vmem_limit_bytes=mb * 2**20)


def layer_norm(x, gain, shift):
    average = jnp.mean(x, axis=-1, keepdims=True)
    centred = x - average
    variance = jnp.mean(centred * centred, axis=-1, keepdims=True)
    return centred * lax.rsqrt(variance + 1e-05) * gain + shift


def bias_range(w, gain, shift):
    w = w.astype(F32)
    middle = jnp.sum(w * shift, axis=1, keepdims=True)
    reach = jnp.sqrt(C * jnp.sum(w * w * gain * gain, axis=1, keepdims=True))
    rounded = jnp.sum(jnp.abs(w * shift), axis=1, keepdims=True)
    return middle, reach * (1 + 1 / 256) + rounded / 256 + 1e-20


def head_weights(own_ref, other_ref):
    own, other = own_ref[...].astype(F32), other_ref[...].astype(F32)
    return jnp.concatenate([own[:2], other[:2], own[4:16]], axis=0)


def encode(x):
    size = jnp.minimum(jnp.abs(x) * LEVELS, LEVELS - 0.01)
    whole = jnp.floor(size)
    code = jnp.exp2(whole - LEVELS / 2) * (1 + (size - whole))
    return jnp.where(x < 0, -code, code)


def decode(code):
    code = code.astype(F32)
    size = jnp.abs(code)
    whole = jnp.floor(jnp.log2(size))
    x = (whole + (LEVELS / 2 - 1) + size * jnp.exp2(-whole)) / LEVELS
    return jnp.where(code < 0, -x, x)


def lay_kernel(where_ref, own_ref, norm_ref, out_ref, picked_ref, normed, held):
    h = where_ref[0]
    first = 6 * where_ref[1] + 3 * h
    gain, shift = norm_ref[0:1], norm_ref[1:2]
    for r in range(3):
        rows = layer_norm(own_ref[3 * h + r].astype(F32), gain, shift)
        normed[r * N : (r + 1) * N, :] = rows.astype(BF16).astype(F32)
        for q in range(3):
            got = normed[pl.ds(r * N + first + q, CHIPS, stride=COLS), :]
            at = r * QR + q * CHIPS
            picked_ref[at : at + CHIPS, :] = got.astype(BF16)
    for r in range(3):
        held[...] = own_ref[3 * (1 - h) + r].astype(F32)
        got = [held[pl.ds(first + q, CHIPS, stride=COLS), :] for q in range(3)]
        at = (3 + r) * QR
        picked_ref[at : at + QR, :] = layer_norm(jnp.concatenate(got, axis=0), gain, shift).astype(BF16)
    for p in range(CHIPS):
        for r in range(3):
            to = (p * 3 + r) * COLS
            out_ref[to : to + COLS, :] = normed[r * N + p * COLS : r * N + (p + 1) * COLS, :]


def lay_out(where, pair, norm):
    return pl.pallas_call(
        lay_kernel,
        in_specs=[SMEM, VMEM, VMEM],
        out_specs=[VMEM, VMEM],
        scratch_shapes=[pltpu.VMEM((3 * N, C), F32), pltpu.VMEM((N, C), F32)],
        out_shape=[
            jax.ShapeDtypeStruct((3 * N, C), F32),
            jax.ShapeDtypeStruct((ROWS * QR, C), BF16),
        ],
        compiler_params=params(24),
        cost_estimate=pl.CostEstimate(flops=20 * N * ROWS * C, bytes_accessed=6 * ROWS * N * C, transcendentals=0),
        name="lay",
    )(where, pair, norm)


def pack_kernel(
    where_ref, laid_ref, picked_ref, other_ref, norm_ref, w_own_ref, w_other_ref, out_ref, held, coded, tail
):
    h = where_ref[0]
    first = 6 * where_ref[1] + 3 * h
    gain, shift = norm_ref[0:1], norm_ref[1:2]
    weights = head_weights(w_own_ref, w_other_ref)
    middle, reach = bias_range(weights, gain, shift)
    entries = []
    for half in range(2):
        entries.append(picked_ref[half * 3 * QR : (half + 1) * 3 * QR, :])
        for r in range(3):
            held[...] = other_ref[3 * (h if half == 0 else 1 - h) + r].astype(F32)
            got = [held[pl.ds(first + q, CHIPS, stride=COLS), :] for q in range(3)]
            entries.append(layer_norm(jnp.concatenate(got, axis=0), gain, shift).astype(BF16))
    entries = jnp.concatenate(entries, axis=0)
    bias = lax.dot_general(weights.astype(BF16), entries, NT, preferred_element_type=F32)
    codes = encode((bias - middle) / reach)
    for at in range(2 * ROWS):
        row = [codes[g : g + 1, at * QR : (at + 1) * QR] for g in range(H)]
        row = jnp.concatenate(row, axis=1)
        for s in range(6):
            coded[at * 6 + s : at * 6 + s + 1, :] = row[:, s * C : (s + 1) * C]
    for p in range(CHIPS):
        y = p // 8 % 4
        tail[p * 24 : p * 24 + 4, :] = laid_ref[p * LAID + 32 : (p + 1) * LAID, :]
        tail[p * 24 + 4 : p * 24 + 4 + SHARE, :] = coded[y * SHARE : (y + 1) * SHARE, :]
        tail[p * 24 + 4 + SHARE : (p + 1) * 24, :] = jnp.zeros((20 - SHARE, C), F32)
    for p in range(CHIPS):
        out_ref[p, :32, :] = laid_ref[p * LAID : p * LAID + 32, :].astype(BF16)
        out_ref[p, 32:, :] = tail[p * 24 : (p + 1) * 24, :].astype(BF16)


def pack(where, laid, picked, other, norm, w_own, w_other):
    return pl.pallas_call(
        pack_kernel,
        in_specs=[SMEM] + [VMEM] * 6,
        out_specs=VMEM,
        scratch_shapes=[
            pltpu.VMEM((N, C), F32),
            pltpu.VMEM((4 * SHARE, C), F32),
            pltpu.VMEM((CHIPS * 24, C), F32),
        ],
        out_shape=jax.ShapeDtypeStruct((CHIPS, MESSAGE, C), BF16),
        compiler_params=params(24),
        cost_estimate=pl.CostEstimate(flops=60 * N * ROWS * C, bytes_accessed=6 * ROWS * N * C, transcendentals=0),
        name="pack",
    )(where, laid, picked, other, norm, w_own, w_other)


def unpack_kernel(arrived_ref, share_ref, column_ref, held):
    held[...] = arrived_ref[...].astype(F32).reshape(CHIPS * MESSAGE, C)
    for j in range(SHARE):
        got = held[pl.ds(LAID + j, CHIPS, stride=MESSAGE), :]
        share_ref[j * CHIPS : (j + 1) * CHIPS, :] = got.astype(BF16)
    for m in range(COLS):
        for r in range(3):
            got = held[pl.ds(r * COLS + m, CHIPS, stride=MESSAGE), :]
            column_ref[m, r * CHIPS : (r + 1) * CHIPS, :] = got.astype(BF16)


def unpack(arrived):
    return pl.pallas_call(
        unpack_kernel,
        out_shape=[
            jax.ShapeDtypeStruct((SHARE * CHIPS, C), BF16),
            jax.ShapeDtypeStruct((COLS, QR, C), BF16),
        ],
        scratch_shapes=[pltpu.VMEM((CHIPS * MESSAGE, C), F32)],
        compiler_params=params(24),
        cost_estimate=pl.CostEstimate(flops=CHIPS * MESSAGE * C, bytes_accessed=8 * CHIPS * MESSAGE * C, transcendentals=0),
        name="unpack",
    )(arrived)


def place_kernel(where_ref, norm_ref, w_own_ref, w_other_ref, part_ref, *refs):
    out_ref = refs[-1]
    reaches = [bias_range(w_ref[...], norm_ref[0:1], norm_ref[1:2])[1] for w_ref in (w_own_ref, w_other_ref)]
    scale = [jnp.broadcast_to(reach[g : g + 1] * ROOT, (8, QR)) for reach in reaches for g in range(2)]
    scale = jnp.concatenate(scale, axis=1)[:1]
    for a in range(3):
        for s in range(6):
            lanes = slice(s * C, (s + 1) * C)
            at = (a * 6 + s) * CHIPS
            out_ref[a * CHIPS : (a + 1) * CHIPS, lanes] = decode(part_ref[at : at + CHIPS, :]) * scale[:, lanes]


def place_bias(where, norm, w_own, w_other, part, step, bias):
    small = lambda g, w: (0, 0)
    in_specs = [
        pl.BlockSpec((2, C), small),
        pl.BlockSpec((16, C), small),
        pl.BlockSpec((16, C), small),
        pl.BlockSpec((SHARE * CHIPS, C), small),
    ]
    operands = [where, norm, w_own, w_other, part]
    aliases = {}
    if bias is not None:
        in_specs.append(pl.BlockSpec(memory_space=pl.ANY))
        operands.append(bias)
        aliases = {5: 0}
    return pl.pallas_call(
        place_kernel,
        grid_spec=pltpu.PrefetchScalarGridSpec(
            num_scalar_prefetch=1,
            grid=(1,),
            in_specs=in_specs,
            out_specs=pl.BlockSpec((QR, 4 * QR), lambda g, w: (lax.rem(w[2] - step + 4, 4), 0)),
        ),
        out_shape=jax.ShapeDtypeStruct((N, 4 * QR), F32),
        input_output_aliases=aliases,
        compiler_params=params(16),
        cost_estimate=pl.CostEstimate(flops=5 * N * N, bytes_accessed=2 * N * N, transcendentals=0),
        name="place",
    )(*operands)


def project_kernel(own_ref, other_ref, wk_ref, wv_ref, keys_ref, values_ref):
    for m in range(GROUP):
        entries = jnp.concatenate([own_ref[m], other_ref[m]], axis=0)
        keys_ref[m] = jnp.dot(entries, wk_ref[...], preferred_element_type=F32).astype(BF16)
        values_ref[m] = lax.dot_general(wv_ref[...], entries, NT, preferred_element_type=F32).astype(BF16)


def project(own, other, wk, wv):
    block = pl.BlockSpec((GROUP, QR, C), lambda m: (m, 0, 0))
    weight = pl.BlockSpec((C, C), lambda m: (0, 0))
    shapes = [(2 * QR, C), (C, 2 * QR)]
    return pl.pallas_call(
        project_kernel,
        grid=(COLS // GROUP,),
        in_specs=[block, block, weight, weight],
        out_specs=[pl.BlockSpec((GROUP,) + shape, lambda m: (m, 0, 0)) for shape in shapes],
        out_shape=[jax.ShapeDtypeStruct((COLS,) + shape, BF16) for shape in shapes],
        compiler_params=params(16),
        cost_estimate=pl.CostEstimate(flops=COLS * 2 * N * C * C, bytes_accessed=10 * N * N, transcendentals=0),
        name="project",
    )(own, other, wk, wv)


def ask_kernel(own_ref, wq_ref, wg_ref, masked_ref, gates_ref):
    head_of_channel = lax.broadcasted_iota(jnp.int32, (C, 2 * QR), 0) // DH
    second = (lax.broadcasted_iota(jnp.int32, (C, 2 * QR), 1) >= QR).astype(jnp.int32)
    first = lax.broadcasted_iota(jnp.int32, (DH, 2 * QR), 1) < QR
    for m in range(GROUP):
        asked = jnp.concatenate([own_ref[m], own_ref[m]], axis=0)
        queries = lax.dot_general(wq_ref[...], asked, NT, preferred_element_type=F32)
        gates = jax.nn.sigmoid(lax.dot_general(wg_ref[...], asked, NT, preferred_element_type=F32))
        for g in range(2):
            lanes = slice(g * 2 * QR, (g + 1) * 2 * QR)
            low, high = slice(2 * g * DH, (2 * g + 1) * DH), slice((2 * g + 1) * DH, (2 * g + 2) * DH)
            masked_ref[m, :, lanes] = jnp.where(head_of_channel == 2 * g + second, queries, 0.0).astype(BF16)
            gates_ref[m, g * DH : (g + 1) * DH, :] = jnp.where(first, gates[low], gates[high]).astype(BF16)


def ask(own, wq, wg):
    weight = pl.BlockSpec((C, C), lambda m: (0, 0))
    shapes = [(C, 4 * QR), (2 * DH, 2 * QR)]
    return pl.pallas_call(
        ask_kernel,
        grid=(COLS // GROUP,),
        in_specs=[pl.BlockSpec((GROUP, QR, C), lambda m: (m, 0, 0)), weight, weight],
        out_specs=[pl.BlockSpec((GROUP,) + shape, lambda m: (m, 0, 0)) for shape in shapes],
        out_shape=[jax.ShapeDtypeStruct((COLS,) + shape, BF16) for shape in shapes],
        compiler_params=params(16),
        cost_estimate=pl.CostEstimate(flops=COLS * 2 * N * C * C, bytes_accessed=10 * N * N, transcendentals=0),
        name="ask",
    )(own, wq, wg)


def attend_kernel(
    k0_ref, v0_ref, far_ref, other_ref, wk_ref, wv_ref, masked_ref, gates_ref, bias_ref, wo_ref, out_ref
):
    first = lax.broadcasted_iota(jnp.int32, (DH, 2 * QR), 1) < QR
    factor = 1.0 / (ROOT * math.log(2.0))

    def project(m):
        entries = jnp.concatenate([far_ref[m], other_ref[m]], axis=0)
        keys = jnp.dot(entries, wk_ref[...], preferred_element_type=F32).astype(BF16)
        values = lax.dot_general(wv_ref[...], entries, NT, preferred_element_type=F32).astype(BF16)
        return jnp.concatenate([k0_ref[m], keys], axis=0), jnp.concatenate([v0_ref[m], values], axis=1)

    def score(m, keys):
        return jnp.dot(keys, masked_ref[m], preferred_element_type=F32) + bias_ref[...]

    def gather(exponent, values):
        totals = jnp.sum(exponent, axis=0, keepdims=True)
        weights = exponent.astype(BF16)
        low = jnp.dot(values[: 2 * DH], weights[:, :256], preferred_element_type=F32)
        both = jnp.dot(values, weights[:, 256:512], preferred_element_type=F32)
        high = jnp.dot(values[2 * DH :], weights[:, 512:], preferred_element_type=F32)
        low = jnp.concatenate([low, both[: 2 * DH, :128]], axis=1)
        high = jnp.concatenate([both[2 * DH :, 128:], high], axis=1)
        return (low, high), totals

    def finish(m, sums, totals):
        gated = []
        for g in range(2):
            lanes = slice(g * 2 * QR, (g + 1) * 2 * QR)
            attended = jnp.where(first, sums[g][:DH], sums[g][DH:]) / totals[:, lanes]
            gated.append(attended * gates_ref[m, g * DH : (g + 1) * DH, :].astype(F32))
        turned = jnp.concatenate(gated, axis=0).T.astype(BF16)
        turned = jnp.concatenate([turned[:QR], turned[QR:]], axis=1)
        out_ref[m] = jnp.dot(turned, wo_ref[...], preferred_element_type=F32).astype(BF16)

    attended = []
    keys, values = project(0)
    scores, held = score(0, keys), values
    keys, values = project(1)
    for m in range(COLS):
        if m + 1 < COLS:
            following, after = score(m + 1, keys), values
        if m + 2 < COLS:
            keys, values = project(m + 2)
        highest = jnp.max(scores, axis=0, keepdims=True)
        attended.append(gather(jnp.exp2((scores - highest) * factor), held))
        if m + 1 < COLS:
            scores, held = following, after
    for m in range(COLS):
        finish(m, *attended[m])


def attend(k0, v0, far, other, wk, wv, masked, gates, bias, wo):
    return pl.pallas_call(
        attend_kernel,
        in_specs=[VMEM] * 10,
        out_specs=VMEM,
        out_shape=jax.ShapeDtypeStruct((COLS, QR, C), BF16),
        compiler_params=params(40),
        cost_estimate=pl.CostEstimate(
            flops=COLS * 8 * N * N * C, bytes_accessed=12 * N * N, transcendentals=COLS * N * N
        ),
        name="attend",
    )(k0, v0, far, other, wk, wv, masked, gates, bias, wo)


def local(pair, ln_gain, ln_shift, w_project, w_bias, w_out):
    swap_heads = functools.partial(lax.ppermute, axis_name="h", perm=[(0, 1), (1, 0)])
    swap_cores = functools.partial(lax.ppermute, axis_name="c", perm=[(0, 1), (1, 0)])
    where = [lax.axis_index(name) for name in ("h", "c", "y", "xl", "z")]
    where = jnp.stack(where).astype(jnp.int32)
    norm = jnp.stack([ln_gain, ln_shift])

    w_own = jnp.pad(w_bias.T, ((0, 14), (0, 0)))
    w_other = swap_heads(w_own)
    laid, picked = lay_out(where, pair, norm)
    blocks = pack(where, laid, picked, swap_cores(pair), norm, w_own, w_other)
    arrived = lax.all_to_all(blocks, CHIP, 0, 0, tiled=True)
    weights = jnp.concatenate([w_project.reshape(C, 4 * 64), w_out.T], axis=1)
    weights_other = swap_heads(weights)
    full = [
        jnp.concatenate([weights[:, t * 64 : (t + 1) * 64], weights_other[:, t * 64 : (t + 1) * 64]], axis=1)
        for t in range(5)
    ]
    wo = full[4].T.reshape(2, 2, DH, C).transpose(1, 0, 2, 3).reshape(C, C)
    full = (full[1], full[2].T, full[0].T, full[3].T, wo)
    arrived, *full = lax.optimization_barrier((arrived, *full))

    wk, wv, wq, wg, wo = full
    share, own = unpack(arrived)
    far = swap_heads(own)
    parts = [share] + [lax.ppermute(share, "y", [(i, (i + o) % 4) for i in range(4)]) for o in (1, 2, 3)]
    masked, gates = ask(own, wq, wg)
    k0, v0 = project(own, swap_cores(own), wk, wv)
    bias = place_bias(where, norm, w_own, w_other, share, 0, None)
    waited = (parts[3], masked, gates, k0, v0, bias)
    parts[3], masked, gates, k0, v0, bias = lax.optimization_barrier(waited)
    for step in (3, 2):
        bias = place_bias(where, norm, w_own, w_other, parts[step], step, bias)
    far, parts[1], bias = lax.optimization_barrier((far, parts[1], bias))
    far_other = swap_cores(far)
    bias = place_bias(where, norm, w_own, w_other, parts[1], 1, bias)
    done = attend(k0, v0, far, far_other, wk, wv, masked, gates, bias, wo)

    sent = done.reshape(COLS, 3, CHIPS, C).transpose(2, 1, 0, 3).reshape(CHIPS, 9, 4, C)
    returned = lax.all_to_all(sent, CHIP, 0, 0, tiled=True)
    return returned.reshape(CHIPS, 3, COLS, C).transpose(1, 0, 2, 3).reshape(3, N, C)


def solution(mesh):
    fine = Mesh(mesh.devices.reshape(2, 4, 8, 2, 2), DAP + ("h",))
    in_specs = (P(DAP, None, None), P(), P(), P(None, None, "h"), P(None, "h"), P("h", None))
    out_specs = P(DAP + ("h",), None, None)
    return jax.shard_map(local, mesh=fine, in_specs=in_specs, out_specs=out_specs, check_vma=False)
```

```python
import functools
import math

import jax
import jax.numpy as jnp
from jax import lax
from jax.experimental import pallas as pl
from jax.experimental.pallas import tpu as pltpu
from jax.sharding import Mesh
from jax.sharding import PartitionSpec as P

F32 = jnp.float32
BF16 = jnp.bfloat16
CHIP = ("xl", "y", "z")
DAP = ("xl", "y", "z", "c")
N, C, H, DH = 768, 128, 4, 32
CHIPS, COLS, ROWS = 64, 12, 6
QR = 3 * CHIPS
KH = ROWS * CHIPS
LEVELS = 240
GROUP = 6
SHARE = 18
LAID = 3 * COLS
MESSAGE = 56
ROOT = math.sqrt(DH)
NT = (((1,), (1,)), ((), ()))
VMEM = pl.BlockSpec(memory_space=pltpu.VMEM)
SMEM = pl.BlockSpec(memory_space=pltpu.SMEM)


def params(mb):
    return pltpu.CompilerParams(vmem_limit_bytes=mb * 2**20)


def layer_norm(x, gain, shift):
    average = jnp.mean(x, axis=-1, keepdims=True)
    centred = x - average
    variance = jnp.mean(centred * centred, axis=-1, keepdims=True)
    return centred * lax.rsqrt(variance + 1e-05) * gain + shift


def bias_range(w, gain, shift):
    w = w.astype(F32)
    middle = jnp.sum(w * shift, axis=1, keepdims=True)
    reach = jnp.sqrt(C * jnp.sum(w * w * gain * gain, axis=1, keepdims=True))
    rounded = jnp.sum(jnp.abs(w * shift), axis=1, keepdims=True)
    return middle, reach * (1 + 1 / 256) + rounded / 256 + 1e-20


def head_weights(own_ref, other_ref):
    own, other = own_ref[...].astype(F32), other_ref[...].astype(F32)
    return jnp.concatenate([own[:2], other[:2], own[4:16]], axis=0)


def encode(x):
    size = jnp.minimum(jnp.abs(x) * LEVELS, LEVELS - 0.01)
    whole = jnp.floor(size)
    code = jnp.exp2(whole - LEVELS / 2) * (1 + (size - whole))
    return jnp.where(x < 0, -code, code)


def decode(code):
    code = code.astype(F32)
    size = jnp.abs(code)
    whole = jnp.floor(jnp.log2(size))
    x = (whole + (LEVELS / 2 - 1) + size * jnp.exp2(-whole)) / LEVELS
    return jnp.where(code < 0, -x, x)


def lay_kernel(where_ref, own_ref, norm_ref, out_ref, picked_ref, normed, held):
    h = where_ref[0]
    first = 6 * where_ref[1] + 3 * h
    gain, shift = norm_ref[0:1], norm_ref[1:2]
    for r in range(3):
        rows = layer_norm(own_ref[3 * h + r].astype(F32), gain, shift)
        normed[r * N : (r + 1) * N, :] = rows.astype(BF16).astype(F32)
        for q in range(3):
            got = normed[pl.ds(r * N + first + q, CHIPS, stride=COLS), :]
            at = r * QR + q * CHIPS
            picked_ref[at : at + CHIPS, :] = got.astype(BF16)
    for r in range(3):
        held[...] = own_ref[3 * (1 - h) + r].astype(F32)
        got = [held[pl.ds(first + q, CHIPS, stride=COLS), :] for q in range(3)]
        at = (3 + r) * QR
        picked_ref[at : at + QR, :] = layer_norm(jnp.concatenate(got, axis=0), gain, shift).astype(BF16)
    for p in range(CHIPS):
        for r in range(3):
            to = (p * 3 + r) * COLS
            out_ref[to : to + COLS, :] = normed[r * N + p * COLS : r * N + (p + 1) * COLS, :]


def lay_out(where, pair, norm):
    return pl.pallas_call(
        lay_kernel,
        in_specs=[SMEM, VMEM, VMEM],
        out_specs=[VMEM, VMEM],
        scratch_shapes=[pltpu.VMEM((3 * N, C), F32), pltpu.VMEM((N, C), F32)],
        out_shape=[
            jax.ShapeDtypeStruct((3 * N, C), F32),
            jax.ShapeDtypeStruct((ROWS * QR, C), BF16),
        ],
        compiler_params=params(24),
        cost_estimate=pl.CostEstimate(flops=20 * N * ROWS * C, bytes_accessed=6 * ROWS * N * C, transcendentals=0),
        name="lay",
    )(where, pair, norm)


def pack_kernel(
    where_ref, laid_ref, picked_ref, other_ref, norm_ref, w_own_ref, w_other_ref, out_ref, held, coded, tail
):
    h = where_ref[0]
    first = 6 * where_ref[1] + 3 * h
    gain, shift = norm_ref[0:1], norm_ref[1:2]
    weights = head_weights(w_own_ref, w_other_ref)
    middle, reach = bias_range(weights, gain, shift)
    entries = []
    for half in range(2):
        entries.append(picked_ref[half * 3 * QR : (half + 1) * 3 * QR, :])
        for r in range(3):
            held[...] = other_ref[3 * (h if half == 0 else 1 - h) + r].astype(F32)
            got = [held[pl.ds(first + q, CHIPS, stride=COLS), :] for q in range(3)]
            entries.append(layer_norm(jnp.concatenate(got, axis=0), gain, shift).astype(BF16))
    entries = jnp.concatenate(entries, axis=0)
    bias = lax.dot_general(weights.astype(BF16), entries, NT, preferred_element_type=F32)
    codes = encode((bias - middle) / reach)
    for at in range(2 * ROWS):
        row = [codes[g : g + 1, at * QR : (at + 1) * QR] for g in range(H)]
        row = jnp.concatenate(row, axis=1)
        for s in range(6):
            coded[at * 6 + s : at * 6 + s + 1, :] = row[:, s * C : (s + 1) * C]
    for p in range(CHIPS):
        y = p // 8 % 4
        tail[p * 24 : p * 24 + 4, :] = laid_ref[p * LAID + 32 : (p + 1) * LAID, :]
        tail[p * 24 + 4 : p * 24 + 4 + SHARE, :] = coded[y * SHARE : (y + 1) * SHARE, :]
        tail[p * 24 + 4 + SHARE : (p + 1) * 24, :] = jnp.zeros((20 - SHARE, C), F32)
    for p in range(CHIPS):
        out_ref[p, :32, :] = laid_ref[p * LAID : p * LAID + 32, :].astype(BF16)
        out_ref[p, 32:, :] = tail[p * 24 : (p + 1) * 24, :].astype(BF16)


def pack(where, laid, picked, other, norm, w_own, w_other):
    return pl.pallas_call(
        pack_kernel,
        in_specs=[SMEM] + [VMEM] * 6,
        out_specs=VMEM,
        scratch_shapes=[
            pltpu.VMEM((N, C), F32),
            pltpu.VMEM((4 * SHARE, C), F32),
            pltpu.VMEM((CHIPS * 24, C), F32),
        ],
        out_shape=jax.ShapeDtypeStruct((CHIPS, MESSAGE, C), BF16),
        compiler_params=params(24),
        cost_estimate=pl.CostEstimate(flops=60 * N * ROWS * C, bytes_accessed=6 * ROWS * N * C, transcendentals=0),
        name="pack",
    )(where, laid, picked, other, norm, w_own, w_other)


def unpack_kernel(arrived_ref, share_ref, column_ref, held):
    held[...] = arrived_ref[...].astype(F32).reshape(CHIPS * MESSAGE, C)
    for j in range(SHARE):
        got = held[pl.ds(LAID + j, CHIPS, stride=MESSAGE), :]
        share_ref[j * CHIPS : (j + 1) * CHIPS, :] = got.astype(BF16)
    for m in range(COLS):
        for r in range(3):
            got = held[pl.ds(r * COLS + m, CHIPS, stride=MESSAGE), :]
            column_ref[m, r * CHIPS : (r + 1) * CHIPS, :] = got.astype(BF16)


def unpack(arrived):
    return pl.pallas_call(
        unpack_kernel,
        out_shape=[
            jax.ShapeDtypeStruct((SHARE * CHIPS, C), BF16),
            jax.ShapeDtypeStruct((COLS, QR, C), BF16),
        ],
        scratch_shapes=[pltpu.VMEM((CHIPS * MESSAGE, C), F32)],
        compiler_params=params(24),
        cost_estimate=pl.CostEstimate(flops=CHIPS * MESSAGE * C, bytes_accessed=8 * CHIPS * MESSAGE * C, transcendentals=0),
        name="unpack",
    )(arrived)


def place_kernel(where_ref, norm_ref, w_own_ref, w_other_ref, part_ref, *refs):
    out_ref = refs[-1]
    reaches = [bias_range(w_ref[...], norm_ref[0:1], norm_ref[1:2])[1] for w_ref in (w_own_ref, w_other_ref)]
    scale = [jnp.broadcast_to(reach[g : g + 1] * ROOT, (8, QR)) for reach in reaches for g in range(2)]
    scale = jnp.concatenate(scale, axis=1)[:1]
    for a in range(3):
        for s in range(6):
            lanes = slice(s * C, (s + 1) * C)
            at = (a * 6 + s) * CHIPS
            out_ref[a * CHIPS : (a + 1) * CHIPS, lanes] = decode(part_ref[at : at + CHIPS, :]) * scale[:, lanes]


def place_bias(where, norm, w_own, w_other, part, step, bias):
    small = lambda g, w: (0, 0)
    in_specs = [
        pl.BlockSpec((2, C), small),
        pl.BlockSpec((16, C), small),
        pl.BlockSpec((16, C), small),
        pl.BlockSpec((SHARE * CHIPS, C), small),
    ]
    operands = [where, norm, w_own, w_other, part]
    aliases = {}
    if bias is not None:
        in_specs.append(pl.BlockSpec(memory_space=pl.ANY))
        operands.append(bias)
        aliases = {5: 0}
    return pl.pallas_call(
        place_kernel,
        grid_spec=pltpu.PrefetchScalarGridSpec(
            num_scalar_prefetch=1,
            grid=(1,),
            in_specs=in_specs,
            out_specs=pl.BlockSpec((QR, 4 * QR), lambda g, w: (lax.rem(w[2] - step + 4, 4), 0)),
        ),
        out_shape=jax.ShapeDtypeStruct((N, 4 * QR), F32),
        input_output_aliases=aliases,
        compiler_params=params(16),
        cost_estimate=pl.CostEstimate(flops=5 * N * N, bytes_accessed=2 * N * N, transcendentals=0),
        name="place",
    )(*operands)


def project_kernel(own_ref, other_ref, wk_ref, wv_ref, keys_ref, values_ref):
    for m in range(GROUP):
        entries = jnp.concatenate([own_ref[m], other_ref[m]], axis=0)
        keys_ref[m] = jnp.dot(entries, wk_ref[...], preferred_element_type=F32).astype(BF16)
        values_ref[m] = lax.dot_general(wv_ref[...], entries, NT, preferred_element_type=F32).astype(BF16)


def project(own, other, wk, wv):
    block = pl.BlockSpec((GROUP, QR, C), lambda m: (m, 0, 0))
    weight = pl.BlockSpec((C, C), lambda m: (0, 0))
    shapes = [(2 * QR, C), (C, 2 * QR)]
    return pl.pallas_call(
        project_kernel,
        grid=(COLS // GROUP,),
        in_specs=[block, block, weight, weight],
        out_specs=[pl.BlockSpec((GROUP,) + shape, lambda m: (m, 0, 0)) for shape in shapes],
        out_shape=[jax.ShapeDtypeStruct((COLS,) + shape, BF16) for shape in shapes],
        compiler_params=params(16),
        cost_estimate=pl.CostEstimate(flops=COLS * 2 * N * C * C, bytes_accessed=10 * N * N, transcendentals=0),
        name="project",
    )(own, other, wk, wv)


def ask_kernel(own_ref, wq_ref, wg_ref, masked_ref, gates_ref):
    head_of_channel = lax.broadcasted_iota(jnp.int32, (C, 2 * QR), 0) // DH
    second = (lax.broadcasted_iota(jnp.int32, (C, 2 * QR), 1) >= QR).astype(jnp.int32)
    first = lax.broadcasted_iota(jnp.int32, (DH, 2 * QR), 1) < QR
    for m in range(GROUP):
        asked = jnp.concatenate([own_ref[m], own_ref[m]], axis=0)
        queries = lax.dot_general(wq_ref[...], asked, NT, preferred_element_type=F32)
        gates = jax.nn.sigmoid(lax.dot_general(wg_ref[...], asked, NT, preferred_element_type=F32))
        for g in range(2):
            lanes = slice(g * 2 * QR, (g + 1) * 2 * QR)
            low, high = slice(2 * g * DH, (2 * g + 1) * DH), slice((2 * g + 1) * DH, (2 * g + 2) * DH)
            masked_ref[m, :, lanes] = jnp.where(head_of_channel == 2 * g + second, queries, 0.0).astype(BF16)
            gates_ref[m, g * DH : (g + 1) * DH, :] = jnp.where(first, gates[low], gates[high]).astype(BF16)


def ask(own, wq, wg):
    weight = pl.BlockSpec((C, C), lambda m: (0, 0))
    shapes = [(C, 4 * QR), (2 * DH, 2 * QR)]
    return pl.pallas_call(
        ask_kernel,
        grid=(COLS // GROUP,),
        in_specs=[pl.BlockSpec((GROUP, QR, C), lambda m: (m, 0, 0)), weight, weight],
        out_specs=[pl.BlockSpec((GROUP,) + shape, lambda m: (m, 0, 0)) for shape in shapes],
        out_shape=[jax.ShapeDtypeStruct((COLS,) + shape, BF16) for shape in shapes],
        compiler_params=params(16),
        cost_estimate=pl.CostEstimate(flops=COLS * 2 * N * C * C, bytes_accessed=10 * N * N, transcendentals=0),
        name="ask",
    )(own, wq, wg)


def attend_kernel(
    k0_ref, v0_ref, far_ref, other_ref, wk_ref, wv_ref, masked_ref, gates_ref, bias_ref, wo_ref, out_ref
):
    first = lax.broadcasted_iota(jnp.int32, (DH, 2 * QR), 1) < QR
    factor = 1.0 / (ROOT * math.log(2.0))

    def project(m):
        entries = jnp.concatenate([far_ref[m], other_ref[m]], axis=0)
        keys = jnp.dot(entries, wk_ref[...], preferred_element_type=F32).astype(BF16)
        values = lax.dot_general(wv_ref[...], entries, NT, preferred_element_type=F32).astype(BF16)
        return jnp.concatenate([k0_ref[m], keys], axis=0), jnp.concatenate([v0_ref[m], values], axis=1)

    def score(m, keys):
        return jnp.dot(keys, masked_ref[m], preferred_element_type=F32) + bias_ref[...]

    def gather(exponent, values):
        totals = jnp.sum(exponent, axis=0, keepdims=True)
        weights = exponent.astype(BF16)
        low = jnp.dot(values[: 2 * DH], weights[:, :256], preferred_element_type=F32)
        both = jnp.dot(values, weights[:, 256:512], preferred_element_type=F32)
        high = jnp.dot(values[2 * DH :], weights[:, 512:], preferred_element_type=F32)
        low = jnp.concatenate([low, both[: 2 * DH, :128]], axis=1)
        high = jnp.concatenate([both[2 * DH :, 128:], high], axis=1)
        return (low, high), totals

    def finish(m, sums, totals):
        gated = []
        for g in range(2):
            lanes = slice(g * 2 * QR, (g + 1) * 2 * QR)
            attended = jnp.where(first, sums[g][:DH], sums[g][DH:]) / totals[:, lanes]
            gated.append(attended * gates_ref[m, g * DH : (g + 1) * DH, :].astype(F32))
        turned = jnp.concatenate(gated, axis=0).T.astype(BF16)
        turned = jnp.concatenate([turned[:QR], turned[QR:]], axis=1)
        out_ref[m] = jnp.dot(turned, wo_ref[...], preferred_element_type=F32).astype(BF16)

    attended = []
    keys, values = project(0)
    scores, held = score(0, keys), values
    keys, values = project(1)
    for m in range(COLS):
        if m + 1 < COLS:
            following, after = score(m + 1, keys), values
        if m + 2 < COLS:
            keys, values = project(m + 2)
        highest = jnp.max(scores, axis=0, keepdims=True)
        attended.append(gather(jnp.exp2((scores - highest) * factor), held))
        if m + 1 < COLS:
            scores, held = following, after
    for m in range(COLS):
        finish(m, *attended[m])


def attend(k0, v0, far, other, wk, wv, masked, gates, bias, wo):
    return pl.pallas_call(
        attend_kernel,
        in_specs=[VMEM] * 10,
        out_specs=VMEM,
        out_shape=jax.ShapeDtypeStruct((COLS, QR, C), BF16),
        compiler_params=params(40),
        cost_estimate=pl.CostEstimate(
            flops=COLS * 8 * N * N * C, bytes_accessed=12 * N * N, transcendentals=COLS * N * N
        ),
        name="attend",
    )(k0, v0, far, other, wk, wv, masked, gates, bias, wo)


def local(pair, ln_gain, ln_shift, w_project, w_bias, w_out):
    swap_heads = functools.partial(lax.ppermute, axis_name="h", perm=[(0, 1), (1, 0)])
    swap_cores = functools.partial(lax.ppermute, axis_name="c", perm=[(0, 1), (1, 0)])
    where = [lax.axis_index(name) for name in ("h", "c", "y", "xl", "z")]
    where = jnp.stack(where).astype(jnp.int32)
    norm = jnp.stack([ln_gain, ln_shift])

    w_own = jnp.pad(w_bias.T, ((0, 14), (0, 0)))
    w_other = swap_heads(w_own)
    laid, picked = lay_out(where, pair, norm)
    blocks = pack(where, laid, picked, swap_cores(pair), norm, w_own, w_other)
    arrived = lax.all_to_all(blocks, CHIP, 0, 0, tiled=True)
    weights = jnp.concatenate([w_project.reshape(C, 4 * 64), w_out.T], axis=1)
    weights_other = swap_heads(weights)
    full = [
        jnp.concatenate([weights[:, t * 64 : (t + 1) * 64], weights_other[:, t * 64 : (t + 1) * 64]], axis=1)
        for t in range(5)
    ]
    wo = full[4].T.reshape(2, 2, DH, C).transpose(1, 0, 2, 3).reshape(C, C)
    full = (full[1], full[2].T, full[0].T, full[3].T, wo)
    arrived, *full = lax.optimization_barrier((arrived, *full))

    wk, wv, wq, wg, wo = full
    share, own = unpack(arrived)
    far = swap_heads(own)
    parts = [share] + [lax.ppermute(share, "y", [(i, (i + o) % 4) for i in range(4)]) for o in (1, 2, 3)]
    masked, gates = ask(own, wq, wg)
    k0, v0 = project(own, swap_cores(own), wk, wv)
    bias = place_bias(where, norm, w_own, w_other, share, 0, None)
    waited = (parts[3], masked, gates, k0, v0, bias)
    parts[3], masked, gates, k0, v0, bias = lax.optimization_barrier(waited)
    for step in (3, 2):
        bias = place_bias(where, norm, w_own, w_other, parts[step], step, bias)
    far, parts[1], bias = lax.optimization_barrier((far, parts[1], bias))
    far_other = swap_cores(far)
    bias = place_bias(where, norm, w_own, w_other, parts[1], 1, bias)
    done = attend(k0, v0, far, far_other, wk, wv, masked, gates, bias, wo)

    sent = done.reshape(COLS, 3, CHIPS, C).transpose(2, 0, 1, 3).reshape(CHIPS, 9, 4, C)
    returned = lax.all_to_all(sent, CHIP, 0, 0, tiled=True)
    return returned.reshape(N, 3, C).transpose(1, 0, 2)


def solution(mesh):
    fine = Mesh(mesh.devices.reshape(2, 4, 8, 2, 2), DAP + ("h",))
    in_specs = (P(DAP, None, None), P(), P(), P(None, None, "h"), P(None, "h"), P("h", None))
    out_specs = P(DAP + ("h",), None, None)
    return jax.shard_map(local, mesh=fine, in_specs=in_specs, out_specs=out_specs, check_vma=False)
```

```python
import functools
import math

import jax
import jax.numpy as jnp
from jax import lax
from jax.experimental import pallas as pl
from jax.experimental.pallas import tpu as pltpu
from jax.sharding import Mesh
from jax.sharding import PartitionSpec as P

F32 = jnp.float32
BF16 = jnp.bfloat16
CHIP = ("xl", "y", "z")
DAP = ("xl", "y", "z", "c")
N, C, H, DH = 768, 128, 4, 32
CHIPS, COLS, ROWS = 64, 12, 6
QR = 3 * CHIPS
KH = ROWS * CHIPS
LEVELS = 240
GROUP = 6
SHARE = 18
LAID = 3 * COLS
MESSAGE = 56
ROOT = math.sqrt(DH)
NT = (((1,), (1,)), ((), ()))
VMEM = pl.BlockSpec(memory_space=pltpu.VMEM)
SMEM = pl.BlockSpec(memory_space=pltpu.SMEM)


def params(mb):
    return pltpu.CompilerParams(vmem_limit_bytes=mb * 2**20)


def layer_norm(x, gain, shift):
    average = jnp.mean(x, axis=-1, keepdims=True)
    centred = x - average
    variance = jnp.mean(centred * centred, axis=-1, keepdims=True)
    return centred * lax.rsqrt(variance + 1e-05) * gain + shift


def bias_range(w, gain, shift):
    w = w.astype(F32)
    middle = jnp.sum(w * shift, axis=1, keepdims=True)
    reach = jnp.sqrt(C * jnp.sum(w * w * gain * gain, axis=1, keepdims=True))
    rounded = jnp.sum(jnp.abs(w * shift), axis=1, keepdims=True)
    return middle, reach * (1 + 1 / 256) + rounded / 256 + 1e-20


def head_weights(own_ref, other_ref):
    own, other = own_ref[...].astype(F32), other_ref[...].astype(F32)
    return jnp.concatenate([own[:2], other[:2], own[4:16]], axis=0)


def encode(x):
    size = jnp.minimum(jnp.abs(x) * LEVELS, LEVELS - 0.01)
    whole = jnp.floor(size)
    code = jnp.exp2(whole - LEVELS / 2) * (1 + (size - whole))
    return jnp.where(x < 0, -code, code)


def decode(code):
    code = code.astype(F32)
    size = jnp.abs(code)
    whole = jnp.floor(jnp.log2(size))
    x = (whole + (LEVELS / 2 - 1) + size * jnp.exp2(-whole)) / LEVELS
    return jnp.where(code < 0, -x, x)


def lay_kernel(where_ref, own_ref, norm_ref, out_ref, picked_ref, normed, held):
    h = where_ref[0]
    first = 6 * where_ref[1] + 3 * h
    gain, shift = norm_ref[0:1], norm_ref[1:2]
    for r in range(3):
        rows = layer_norm(own_ref[3 * h + r].astype(F32), gain, shift)
        normed[r * N : (r + 1) * N, :] = rows.astype(BF16).astype(F32)
        for q in range(3):
            got = normed[pl.ds(r * N + first + q, CHIPS, stride=COLS), :]
            at = r * QR + q * CHIPS
            picked_ref[at : at + CHIPS, :] = got.astype(BF16)
    for r in range(3):
        held[:N, :] = own_ref[3 * (1 - h) + r].astype(F32)
        got = [held[pl.ds(first + q, CHIPS, stride=COLS), :] for q in range(3)]
        at = (3 + r) * QR
        picked_ref[at : at + QR, :] = layer_norm(jnp.concatenate(got, axis=0), gain, shift).astype(BF16)
    for p in range(CHIPS):
        for r in range(3):
            to = (p * 3 + r) * COLS
            out_ref[to : to + COLS, :] = normed[r * N + p * COLS : r * N + (p + 1) * COLS, :]


def lay_out(where, pair, norm):
    return pl.pallas_call(
        lay_kernel,
        in_specs=[SMEM, VMEM, VMEM],
        out_specs=[VMEM, VMEM],
        scratch_shapes=[pltpu.VMEM((3 * N + 16, C), F32), pltpu.VMEM((N + 16, C), F32)],
        out_shape=[
            jax.ShapeDtypeStruct((3 * N, C), F32),
            jax.ShapeDtypeStruct((ROWS * QR, C), BF16),
        ],
        compiler_params=params(24),
        cost_estimate=pl.CostEstimate(flops=20 * N * ROWS * C, bytes_accessed=6 * ROWS * N * C, transcendentals=0),
        name="lay",
    )(where, pair, norm)


def pack_kernel(
    where_ref, laid_ref, picked_ref, other_ref, norm_ref, w_own_ref, w_other_ref, out_ref, held, coded, tail
):
    h = where_ref[0]
    first = 6 * where_ref[1] + 3 * h
    gain, shift = norm_ref[0:1], norm_ref[1:2]
    weights = head_weights(w_own_ref, w_other_ref)
    middle, reach = bias_range(weights, gain, shift)
    entries = []
    for half in range(2):
        entries.append(picked_ref[half * 3 * QR : (half + 1) * 3 * QR, :])
        for r in range(3):
            held[:N, :] = other_ref[3 * (h if half == 0 else 1 - h) + r].astype(F32)
            got = [held[pl.ds(first + q, CHIPS, stride=COLS), :] for q in range(3)]
            entries.append(layer_norm(jnp.concatenate(got, axis=0), gain, shift).astype(BF16))
    entries = jnp.concatenate(entries, axis=0)
    bias = lax.dot_general(weights.astype(BF16), entries, NT, preferred_element_type=F32)
    codes = encode((bias - middle) / reach)
    for at in range(2 * ROWS):
        row = [codes[g : g + 1, at * QR : (at + 1) * QR] for g in range(H)]
        row = jnp.concatenate(row, axis=1)
        for s in range(6):
            coded[at * 6 + s : at * 6 + s + 1, :] = row[:, s * C : (s + 1) * C]
    for p in range(CHIPS):
        y = p // 8 % 4
        tail[p * 24 : p * 24 + 4, :] = laid_ref[p * LAID + 32 : (p + 1) * LAID, :]
        tail[p * 24 + 4 : p * 24 + 4 + SHARE, :] = coded[y * SHARE : (y + 1) * SHARE, :]
        tail[p * 24 + 4 + SHARE : (p + 1) * 24, :] = jnp.zeros((20 - SHARE, C), F32)
    for p in range(CHIPS):
        out_ref[p, :32, :] = laid_ref[p * LAID : p * LAID + 32, :].astype(BF16)
        out_ref[p, 32:, :] = tail[p * 24 : (p + 1) * 24, :].astype(BF16)


def pack(where, laid, picked, other, norm, w_own, w_other):
    return pl.pallas_call(
        pack_kernel,
        in_specs=[SMEM] + [VMEM] * 6,
        out_specs=VMEM,
        scratch_shapes=[
            pltpu.VMEM((N + 16, C), F32),
            pltpu.VMEM((4 * SHARE, C), F32),
            pltpu.VMEM((CHIPS * 24, C), F32),
        ],
        out_shape=jax.ShapeDtypeStruct((CHIPS, MESSAGE, C), BF16),
        compiler_params=params(24),
        cost_estimate=pl.CostEstimate(flops=60 * N * ROWS * C, bytes_accessed=6 * ROWS * N * C, transcendentals=0),
        name="pack",
    )(where, laid, picked, other, norm, w_own, w_other)


def unpack_kernel(arrived_ref, share_ref, column_ref, held):
    held[...] = arrived_ref[...].astype(F32).reshape(CHIPS * MESSAGE, C)
    for j in range(SHARE):
        got = held[pl.ds(LAID + j, CHIPS, stride=MESSAGE), :]
        share_ref[j * CHIPS : (j + 1) * CHIPS, :] = got.astype(BF16)
    for m in range(COLS):
        for r in range(3):
            got = held[pl.ds(r * COLS + m, CHIPS, stride=MESSAGE), :]
            column_ref[m, r * CHIPS : (r + 1) * CHIPS, :] = got.astype(BF16)


def unpack(arrived):
    return pl.pallas_call(
        unpack_kernel,
        out_shape=[
            jax.ShapeDtypeStruct((SHARE * CHIPS, C), BF16),
            jax.ShapeDtypeStruct((COLS, QR, C), BF16),
        ],
        scratch_shapes=[pltpu.VMEM((CHIPS * MESSAGE, C), F32)],
        compiler_params=params(24),
        cost_estimate=pl.CostEstimate(flops=CHIPS * MESSAGE * C, bytes_accessed=8 * CHIPS * MESSAGE * C, transcendentals=0),
        name="unpack",
    )(arrived)


def place_kernel(where_ref, norm_ref, w_own_ref, w_other_ref, part_ref, *refs):
    out_ref = refs[-1]
    reaches = [bias_range(w_ref[...], norm_ref[0:1], norm_ref[1:2])[1] for w_ref in (w_own_ref, w_other_ref)]
    scale = [jnp.broadcast_to(reach[g : g + 1] * ROOT, (8, QR)) for reach in reaches for g in range(2)]
    scale = jnp.concatenate(scale, axis=1)[:1]
    for a in range(3):
        for s in range(6):
            lanes = slice(s * C, (s + 1) * C)
            at = (a * 6 + s) * CHIPS
            out_ref[a * CHIPS : (a + 1) * CHIPS, lanes] = decode(part_ref[at : at + CHIPS, :]) * scale[:, lanes]


def place_bias(where, norm, w_own, w_other, part, step, bias):
    small = lambda g, w: (0, 0)
    in_specs = [
        pl.BlockSpec((2, C), small),
        pl.BlockSpec((16, C), small),
        pl.BlockSpec((16, C), small),
        pl.BlockSpec((SHARE * CHIPS, C), small),
    ]
    operands = [where, norm, w_own, w_other, part]
    aliases = {}
    if bias is not None:
        in_specs.append(pl.BlockSpec(memory_space=pl.ANY))
        operands.append(bias)
        aliases = {5: 0}
    return pl.pallas_call(
        place_kernel,
        grid_spec=pltpu.PrefetchScalarGridSpec(
            num_scalar_prefetch=1,
            grid=(1,),
            in_specs=in_specs,
            out_specs=pl.BlockSpec((QR, 4 * QR), lambda g, w: (lax.rem(w[2] - step + 4, 4), 0)),
        ),
        out_shape=jax.ShapeDtypeStruct((N, 4 * QR), F32),
        input_output_aliases=aliases,
        compiler_params=params(16),
        cost_estimate=pl.CostEstimate(flops=5 * N * N, bytes_accessed=2 * N * N, transcendentals=0),
        name="place",
    )(*operands)


def project_kernel(own_ref, other_ref, wk_ref, wv_ref, keys_ref, values_ref):
    for m in range(GROUP):
        entries = jnp.concatenate([own_ref[m], other_ref[m]], axis=0)
        keys_ref[m] = jnp.dot(entries, wk_ref[...], preferred_element_type=F32).astype(BF16)
        values_ref[m] = lax.dot_general(wv_ref[...], entries, NT, preferred_element_type=F32).astype(BF16)


def project(own, other, wk, wv):
    block = pl.BlockSpec((GROUP, QR, C), lambda m: (m, 0, 0))
    weight = pl.BlockSpec((C, C), lambda m: (0, 0))
    shapes = [(2 * QR, C), (C, 2 * QR)]
    return pl.pallas_call(
        project_kernel,
        grid=(COLS // GROUP,),
        in_specs=[block, block, weight, weight],
        out_specs=[pl.BlockSpec((GROUP,) + shape, lambda m: (m, 0, 0)) for shape in shapes],
        out_shape=[jax.ShapeDtypeStruct((COLS,) + shape, BF16) for shape in shapes],
        compiler_params=params(16),
        cost_estimate=pl.CostEstimate(flops=COLS * 2 * N * C * C, bytes_accessed=10 * N * N, transcendentals=0),
        name="project",
    )(own, other, wk, wv)


def ask_kernel(own_ref, wq_ref, wg_ref, masked_ref, gates_ref):
    head_of_channel = lax.broadcasted_iota(jnp.int32, (C, 2 * QR), 0) // DH
    second = (lax.broadcasted_iota(jnp.int32, (C, 2 * QR), 1) >= QR).astype(jnp.int32)
    first = lax.broadcasted_iota(jnp.int32, (DH, 2 * QR), 1) < QR
    for m in range(GROUP):
        asked = jnp.concatenate([own_ref[m], own_ref[m]], axis=0)
        queries = lax.dot_general(wq_ref[...], asked, NT, preferred_element_type=F32)
        gates = jax.nn.sigmoid(lax.dot_general(wg_ref[...], asked, NT, preferred_element_type=F32))
        for g in range(2):
            lanes = slice(g * 2 * QR, (g + 1) * 2 * QR)
            low, high = slice(2 * g * DH, (2 * g + 1) * DH), slice((2 * g + 1) * DH, (2 * g + 2) * DH)
            masked_ref[m, :, lanes] = jnp.where(head_of_channel == 2 * g + second, queries, 0.0).astype(BF16)
            gates_ref[m, g * DH : (g + 1) * DH, :] = jnp.where(first, gates[low], gates[high]).astype(BF16)


def ask(own, wq, wg):
    weight = pl.BlockSpec((C, C), lambda m: (0, 0))
    shapes = [(C, 4 * QR), (2 * DH, 2 * QR)]
    return pl.pallas_call(
        ask_kernel,
        grid=(COLS // GROUP,),
        in_specs=[pl.BlockSpec((GROUP, QR, C), lambda m: (m, 0, 0)), weight, weight],
        out_specs=[pl.BlockSpec((GROUP,) + shape, lambda m: (m, 0, 0)) for shape in shapes],
        out_shape=[jax.ShapeDtypeStruct((COLS,) + shape, BF16) for shape in shapes],
        compiler_params=params(16),
        cost_estimate=pl.CostEstimate(flops=COLS * 2 * N * C * C, bytes_accessed=10 * N * N, transcendentals=0),
        name="ask",
    )(own, wq, wg)


def attend_kernel(
    k0_ref, v0_ref, far_ref, other_ref, wk_ref, wv_ref, masked_ref, gates_ref, bias_ref, wo_ref, out_ref
):
    first = lax.broadcasted_iota(jnp.int32, (DH, 2 * QR), 1) < QR
    factor = 1.0 / (ROOT * math.log(2.0))

    def project(m):
        entries = jnp.concatenate([far_ref[m], other_ref[m]], axis=0)
        keys = jnp.dot(entries, wk_ref[...], preferred_element_type=F32).astype(BF16)
        values = lax.dot_general(wv_ref[...], entries, NT, preferred_element_type=F32).astype(BF16)
        return jnp.concatenate([k0_ref[m], keys], axis=0), jnp.concatenate([v0_ref[m], values], axis=1)

    def score(m, keys):
        return jnp.dot(keys, masked_ref[m], preferred_element_type=F32) + bias_ref[...]

    def gather(exponent, values):
        totals = jnp.sum(exponent, axis=0, keepdims=True)
        weights = exponent.astype(BF16)
        low = jnp.dot(values[: 2 * DH], weights[:, :256], preferred_element_type=F32)
        both = jnp.dot(values, weights[:, 256:512], preferred_element_type=F32)
        high = jnp.dot(values[2 * DH :], weights[:, 512:], preferred_element_type=F32)
        low = jnp.concatenate([low, both[: 2 * DH, :128]], axis=1)
        high = jnp.concatenate([both[2 * DH :, 128:], high], axis=1)
        return (low, high), totals

    def finish(m, sums, totals):
        gated = []
        for g in range(2):
            lanes = slice(g * 2 * QR, (g + 1) * 2 * QR)
            attended = jnp.where(first, sums[g][:DH], sums[g][DH:]) / totals[:, lanes]
            gated.append(attended * gates_ref[m, g * DH : (g + 1) * DH, :].astype(F32))
        turned = jnp.concatenate(gated, axis=0).T.astype(BF16)
        turned = jnp.concatenate([turned[:QR], turned[QR:]], axis=1)
        out_ref[m] = jnp.dot(turned, wo_ref[...], preferred_element_type=F32).astype(BF16)

    attended = []
    keys, values = project(0)
    scores, held = score(0, keys), values
    keys, values = project(1)
    for m in range(COLS):
        if m + 1 < COLS:
            following, after = score(m + 1, keys), values
        if m + 2 < COLS:
            keys, values = project(m + 2)
        highest = jnp.max(scores, axis=0, keepdims=True)
        attended.append(gather(jnp.exp2((scores - highest) * factor), held))
        if m + 1 < COLS:
            scores, held = following, after
    for m in range(COLS):
        finish(m, *attended[m])


def attend(k0, v0, far, other, wk, wv, masked, gates, bias, wo):
    return pl.pallas_call(
        attend_kernel,
        in_specs=[VMEM] * 10,
        out_specs=VMEM,
        out_shape=jax.ShapeDtypeStruct((COLS, QR, C), BF16),
        compiler_params=params(40),
        cost_estimate=pl.CostEstimate(
            flops=COLS * 8 * N * N * C, bytes_accessed=12 * N * N, transcendentals=COLS * N * N
        ),
        name="attend",
    )(k0, v0, far, other, wk, wv, masked, gates, bias, wo)


def local(pair, ln_gain, ln_shift, w_project, w_bias, w_out):
    swap_heads = functools.partial(lax.ppermute, axis_name="h", perm=[(0, 1), (1, 0)])
    swap_cores = functools.partial(lax.ppermute, axis_name="c", perm=[(0, 1), (1, 0)])
    where = [lax.axis_index(name) for name in ("h", "c", "y", "xl", "z")]
    where = jnp.stack(where).astype(jnp.int32)
    norm = jnp.stack([ln_gain, ln_shift])

    w_own = jnp.pad(w_bias.T, ((0, 14), (0, 0)))
    w_other = swap_heads(w_own)
    laid, picked = lay_out(where, pair, norm)
    blocks = pack(where, laid, picked, swap_cores(pair), norm, w_own, w_other)
    arrived = lax.all_to_all(blocks, CHIP, 0, 0, tiled=True)
    weights = jnp.concatenate([w_project.reshape(C, 4 * 64), w_out.T], axis=1)
    weights_other = swap_heads(weights)
    full = [
        jnp.concatenate([weights[:, t * 64 : (t + 1) * 64], weights_other[:, t * 64 : (t + 1) * 64]], axis=1)
        for t in range(5)
    ]
    wo = full[4].T.reshape(2, 2, DH, C).transpose(1, 0, 2, 3).reshape(C, C)
    full = (full[1], full[2].T, full[0].T, full[3].T, wo)
    arrived, *full = lax.optimization_barrier((arrived, *full))

    wk, wv, wq, wg, wo = full
    share, own = unpack(arrived)
    far = swap_heads(own)
    parts = [share] + [lax.ppermute(share, "y", [(i, (i + o) % 4) for i in range(4)]) for o in (1, 2, 3)]
    masked, gates = ask(own, wq, wg)
    k0, v0 = project(own, swap_cores(own), wk, wv)
    bias = place_bias(where, norm, w_own, w_other, share, 0, None)
    waited = (parts[3], masked, gates, k0, v0, bias)
    parts[3], masked, gates, k0, v0, bias = lax.optimization_barrier(waited)
    for step in (3, 2):
        bias = place_bias(where, norm, w_own, w_other, parts[step], step, bias)
    far, parts[1], bias = lax.optimization_barrier((far, parts[1], bias))
    far_other = swap_cores(far)
    bias = place_bias(where, norm, w_own, w_other, parts[1], 1, bias)
    done = attend(k0, v0, far, far_other, wk, wv, masked, gates, bias, wo)

    sent = done.reshape(COLS, 3, CHIPS, C).transpose(2, 0, 1, 3).reshape(CHIPS, 9, 4, C)
    returned = lax.all_to_all(sent, CHIP, 0, 0, tiled=True)
    return returned.reshape(N, 3, C).transpose(1, 0, 2)


def solution(mesh):
    fine = Mesh(mesh.devices.reshape(2, 4, 8, 2, 2), DAP + ("h",))
    in_specs = (P(DAP, None, None), P(), P(), P(None, None, "h"), P(None, "h"), P("h", None))
    out_specs = P(DAP + ("h",), None, None)
    return jax.shard_map(local, mesh=fine, in_specs=in_specs, out_specs=out_specs, check_vma=False)
```

```python
import functools
import math

import jax
import jax.numpy as jnp
from jax import lax
from jax.experimental import pallas as pl
from jax.experimental.pallas import tpu as pltpu
from jax.sharding import Mesh
from jax.sharding import PartitionSpec as P

F32 = jnp.float32
BF16 = jnp.bfloat16
CHIP = ("xl", "y", "z")
DAP = ("xl", "y", "z", "c")
N, C, H, DH = 768, 128, 4, 32
CHIPS, COLS, ROWS = 64, 12, 6
QR = 3 * CHIPS
KH = ROWS * CHIPS
LEVELS = 240
GROUP = 6
SHARE = 18
LAID = 3 * COLS
MESSAGE = 56
ROOT = math.sqrt(DH)
NT = (((1,), (1,)), ((), ()))
VMEM = pl.BlockSpec(memory_space=pltpu.VMEM)
SMEM = pl.BlockSpec(memory_space=pltpu.SMEM)


def params(mb):
    return pltpu.CompilerParams(vmem_limit_bytes=mb * 2**20)


def layer_norm(x, gain, shift):
    average = jnp.mean(x, axis=-1, keepdims=True)
    centred = x - average
    variance = jnp.mean(centred * centred, axis=-1, keepdims=True)
    return centred * lax.rsqrt(variance + 1e-05) * gain + shift


def bias_range(w, gain, shift):
    w = w.astype(F32)
    middle = jnp.sum(w * shift, axis=1, keepdims=True)
    reach = jnp.sqrt(C * jnp.sum(w * w * gain * gain, axis=1, keepdims=True))
    rounded = jnp.sum(jnp.abs(w * shift), axis=1, keepdims=True)
    return middle, reach * (1 + 1 / 256) + rounded / 256 + 1e-20


def head_weights(own_ref, other_ref):
    own, other = own_ref[...].astype(F32), other_ref[...].astype(F32)
    return jnp.concatenate([own[:2], other[:2], own[4:16]], axis=0)


def encode(x):
    size = jnp.minimum(jnp.abs(x) * LEVELS, LEVELS - 0.01)
    whole = jnp.floor(size)
    code = jnp.exp2(whole - LEVELS / 2) * (1 + (size - whole))
    return jnp.where(x < 0, -code, code)


def decode(code):
    code = code.astype(F32)
    size = jnp.abs(code)
    whole = jnp.floor(jnp.log2(size))
    x = (whole + (LEVELS / 2 - 1) + size * jnp.exp2(-whole)) / LEVELS
    return jnp.where(code < 0, -x, x)


def lay_kernel(where_ref, own_ref, norm_ref, out_ref, picked_ref, normed, held):
    h = where_ref[0]
    first = 6 * where_ref[1] + 3 * h
    gain, shift = norm_ref[0:1], norm_ref[1:2]
    for r in range(3):
        rows = layer_norm(own_ref[3 * h + r].astype(F32), gain, shift)
        normed[r * N : (r + 1) * N, :] = rows.astype(BF16).astype(F32)
        for q in range(3):
            got = normed[pl.ds(r * N + first + q, CHIPS, stride=COLS), :]
            at = r * QR + q * CHIPS
            picked_ref[at : at + CHIPS, :] = got.astype(BF16)
    for r in range(3):
        held[:N, :] = own_ref[3 * (1 - h) + r].astype(F32)
        got = [held[pl.ds(first + q, CHIPS, stride=COLS), :] for q in range(3)]
        at = (3 + r) * QR
        picked_ref[at : at + QR, :] = layer_norm(jnp.concatenate(got, axis=0), gain, shift).astype(BF16)
    for p in range(CHIPS):
        for r in range(3):
            to = (p * 3 + r) * COLS
            out_ref[to : to + COLS, :] = normed[r * N + p * COLS : r * N + (p + 1) * COLS, :]


def lay_out(where, pair, norm):
    return pl.pallas_call(
        lay_kernel,
        in_specs=[SMEM, VMEM, VMEM],
        out_specs=[VMEM, VMEM],
        scratch_shapes=[pltpu.VMEM((3 * N + 16, C), F32), pltpu.VMEM((N + 16, C), F32)],
        out_shape=[
            jax.ShapeDtypeStruct((3 * N, C), F32),
            jax.ShapeDtypeStruct((ROWS * QR, C), BF16),
        ],
        compiler_params=params(24),
        cost_estimate=pl.CostEstimate(flops=20 * N * ROWS * C, bytes_accessed=6 * ROWS * N * C, transcendentals=0),
        name="lay",
    )(where, pair, norm)


def pack_kernel(
    where_ref, laid_ref, picked_ref, other_ref, norm_ref, w_own_ref, w_other_ref, out_ref, held, coded, tail
):
    h = where_ref[0]
    first = 6 * where_ref[1] + 3 * h
    gain, shift = norm_ref[0:1], norm_ref[1:2]
    weights = head_weights(w_own_ref, w_other_ref)
    middle, reach = bias_range(weights, gain, shift)
    entries = []
    for half in range(2):
        entries.append(picked_ref[half * 3 * QR : (half + 1) * 3 * QR, :])
        for r in range(3):
            held[:N, :] = other_ref[3 * (h if half == 0 else 1 - h) + r].astype(F32)
            got = [held[pl.ds(first + q, CHIPS, stride=COLS), :] for q in range(3)]
            entries.append(layer_norm(jnp.concatenate(got, axis=0), gain, shift).astype(BF16))
    entries = jnp.concatenate(entries, axis=0)
    bias = lax.dot_general(weights.astype(BF16), entries, NT, preferred_element_type=F32)
    codes = encode((bias - middle) / reach)
    for at in range(2 * ROWS):
        row = [codes[g : g + 1, at * QR : (at + 1) * QR] for g in range(H)]
        row = jnp.concatenate(row, axis=1)
        for s in range(6):
            coded[at * 6 + s : at * 6 + s + 1, :] = row[:, s * C : (s + 1) * C]
    for p in range(CHIPS):
        y = p // 8 % 4
        tail[p * 24 : p * 24 + 4, :] = laid_ref[p * LAID + 32 : (p + 1) * LAID, :]
        tail[p * 24 + 4 : p * 24 + 4 + SHARE, :] = coded[y * SHARE : (y + 1) * SHARE, :]
        tail[p * 24 + 4 + SHARE : (p + 1) * 24, :] = jnp.zeros((20 - SHARE, C), F32)
    for p in range(CHIPS):
        out_ref[p, :32, :] = laid_ref[p * LAID : p * LAID + 32, :].astype(BF16)
        out_ref[p, 32:, :] = tail[p * 24 : (p + 1) * 24, :].astype(BF16)


def pack(where, laid, picked, other, norm, w_own, w_other):
    return pl.pallas_call(
        pack_kernel,
        in_specs=[SMEM] + [VMEM] * 6,
        out_specs=VMEM,
        scratch_shapes=[
            pltpu.VMEM((N + 16, C), F32),
            pltpu.VMEM((4 * SHARE, C), F32),
            pltpu.VMEM((CHIPS * 24, C), F32),
        ],
        out_shape=jax.ShapeDtypeStruct((CHIPS, MESSAGE, C), BF16),
        compiler_params=params(24),
        cost_estimate=pl.CostEstimate(flops=60 * N * ROWS * C, bytes_accessed=6 * ROWS * N * C, transcendentals=0),
        name="pack",
    )(where, laid, picked, other, norm, w_own, w_other)


def unpack_kernel(arrived_ref, share_ref, column_ref, held):
    held[...] = arrived_ref[...].astype(F32).reshape(CHIPS * MESSAGE, C)
    for j in range(SHARE):
        got = held[pl.ds(LAID + j, CHIPS, stride=MESSAGE), :]
        share_ref[j * CHIPS : (j + 1) * CHIPS, :] = got.astype(BF16)
    for m in range(COLS):
        for r in range(3):
            got = held[pl.ds(r * COLS + m, CHIPS, stride=MESSAGE), :]
            column_ref[m, r * CHIPS : (r + 1) * CHIPS, :] = got.astype(BF16)


def unpack(arrived):
    return pl.pallas_call(
        unpack_kernel,
        out_shape=[
            jax.ShapeDtypeStruct((SHARE * CHIPS, C), BF16),
            jax.ShapeDtypeStruct((COLS, QR, C), BF16),
        ],
        scratch_shapes=[pltpu.VMEM((CHIPS * MESSAGE, C), F32)],
        compiler_params=params(24),
        cost_estimate=pl.CostEstimate(flops=CHIPS * MESSAGE * C, bytes_accessed=8 * CHIPS * MESSAGE * C, transcendentals=0),
        name="unpack",
    )(arrived)


def place_kernel(step, where_ref, norm_ref, w_own_ref, w_other_ref, part_ref, *refs):
    out_ref = refs[-1]
    reaches = [bias_range(w_ref[...], norm_ref[0:1], norm_ref[1:2])[1] for w_ref in (w_own_ref, w_other_ref)]
    scale = [jnp.broadcast_to(reach[g : g + 1] * ROOT, (8, QR)) for reach in reaches for g in range(2)]
    scale = jnp.concatenate(scale, axis=1)[:1]
    quarter = lax.rem(where_ref[2] - step + 4, 4) * QR
    for a in range(3):
        to = pl.multiple_of(quarter + a * CHIPS, CHIPS)
        for s in range(6):
            lanes = slice(s * C, (s + 1) * C)
            at = (a * 6 + s) * CHIPS
            out_ref[pl.ds(to, CHIPS), lanes] = decode(part_ref[at : at + CHIPS, :]) * scale[:, lanes]


def place_bias(where, norm, w_own, w_other, part, step, bias):
    operands = [where, norm, w_own, w_other, part] + ([] if bias is None else [bias])
    return pl.pallas_call(
        functools.partial(place_kernel, step),
        in_specs=[SMEM] + [VMEM] * (len(operands) - 1),
        out_specs=VMEM,
        out_shape=jax.ShapeDtypeStruct((N, 4 * QR), F32),
        input_output_aliases={} if bias is None else {5: 0},
        compiler_params=params(16),
        cost_estimate=pl.CostEstimate(flops=5 * N * N, bytes_accessed=2 * N * N, transcendentals=0),
        name="place",
    )(*operands)


def project_kernel(own_ref, other_ref, wk_ref, wv_ref, keys_ref, values_ref):
    for m in range(GROUP):
        entries = jnp.concatenate([own_ref[m], other_ref[m]], axis=0)
        keys_ref[m] = jnp.dot(entries, wk_ref[...], preferred_element_type=F32).astype(BF16)
        values_ref[m] = lax.dot_general(wv_ref[...], entries, NT, preferred_element_type=F32).astype(BF16)


def project(own, other, wk, wv):
    block = pl.BlockSpec((GROUP, QR, C), lambda m: (m, 0, 0))
    weight = pl.BlockSpec((C, C), lambda m: (0, 0))
    shapes = [(2 * QR, C), (C, 2 * QR)]
    return pl.pallas_call(
        project_kernel,
        grid=(COLS // GROUP,),
        in_specs=[block, block, weight, weight],
        out_specs=[pl.BlockSpec((GROUP,) + shape, lambda m: (m, 0, 0)) for shape in shapes],
        out_shape=[jax.ShapeDtypeStruct((COLS,) + shape, BF16) for shape in shapes],
        compiler_params=params(16),
        cost_estimate=pl.CostEstimate(flops=COLS * 2 * N * C * C, bytes_accessed=10 * N * N, transcendentals=0),
        name="project",
    )(own, other, wk, wv)


def ask_kernel(own_ref, wq_ref, wg_ref, masked_ref, gates_ref):
    head_of_channel = lax.broadcasted_iota(jnp.int32, (C, 2 * QR), 0) // DH
    second = (lax.broadcasted_iota(jnp.int32, (C, 2 * QR), 1) >= QR).astype(jnp.int32)
    first = lax.broadcasted_iota(jnp.int32, (DH, 2 * QR), 1) < QR
    for m in range(GROUP):
        asked = jnp.concatenate([own_ref[m], own_ref[m]], axis=0)
        queries = lax.dot_general(wq_ref[...], asked, NT, preferred_element_type=F32)
        gates = jax.nn.sigmoid(lax.dot_general(wg_ref[...], asked, NT, preferred_element_type=F32))
        for g in range(2):
            lanes = slice(g * 2 * QR, (g + 1) * 2 * QR)
            low, high = slice(2 * g * DH, (2 * g + 1) * DH), slice((2 * g + 1) * DH, (2 * g + 2) * DH)
            masked_ref[m, :, lanes] = jnp.where(head_of_channel == 2 * g + second, queries, 0.0).astype(BF16)
            gates_ref[m, g * DH : (g + 1) * DH, :] = jnp.where(first, gates[low], gates[high]).astype(BF16)


def ask(own, wq, wg):
    weight = pl.BlockSpec((C, C), lambda m: (0, 0))
    shapes = [(C, 4 * QR), (2 * DH, 2 * QR)]
    return pl.pallas_call(
        ask_kernel,
        grid=(COLS // GROUP,),
        in_specs=[pl.BlockSpec((GROUP, QR, C), lambda m: (m, 0, 0)), weight, weight],
        out_specs=[pl.BlockSpec((GROUP,) + shape, lambda m: (m, 0, 0)) for shape in shapes],
        out_shape=[jax.ShapeDtypeStruct((COLS,) + shape, BF16) for shape in shapes],
        compiler_params=params(16),
        cost_estimate=pl.CostEstimate(flops=COLS * 2 * N * C * C, bytes_accessed=10 * N * N, transcendentals=0),
        name="ask",
    )(own, wq, wg)


def attend_kernel(
    k0_ref, v0_ref, far_ref, other_ref, wk_ref, wv_ref, masked_ref, gates_ref, bias_ref, wo_ref, out_ref
):
    first = lax.broadcasted_iota(jnp.int32, (DH, 2 * QR), 1) < QR
    factor = 1.0 / (ROOT * math.log(2.0))

    def project(m):
        entries = jnp.concatenate([far_ref[m], other_ref[m]], axis=0)
        keys = jnp.dot(entries, wk_ref[...], preferred_element_type=F32).astype(BF16)
        values = lax.dot_general(wv_ref[...], entries, NT, preferred_element_type=F32).astype(BF16)
        return jnp.concatenate([k0_ref[m], keys], axis=0), jnp.concatenate([v0_ref[m], values], axis=1)

    def score(m, keys):
        return jnp.dot(keys, masked_ref[m], preferred_element_type=F32) + bias_ref[...]

    def gather(exponent, values):
        totals = jnp.sum(exponent, axis=0, keepdims=True)
        weights = exponent.astype(BF16)
        low = jnp.dot(values[: 2 * DH], weights[:, :256], preferred_element_type=F32)
        both = jnp.dot(values, weights[:, 256:512], preferred_element_type=F32)
        high = jnp.dot(values[2 * DH :], weights[:, 512:], preferred_element_type=F32)
        low = jnp.concatenate([low, both[: 2 * DH, :128]], axis=1)
        high = jnp.concatenate([both[2 * DH :, 128:], high], axis=1)
        return (low, high), totals

    def finish(m, sums, totals):
        gated = []
        for g in range(2):
            lanes = slice(g * 2 * QR, (g + 1) * 2 * QR)
            attended = jnp.where(first, sums[g][:DH], sums[g][DH:]) / totals[:, lanes]
            gated.append(attended * gates_ref[m, g * DH : (g + 1) * DH, :].astype(F32))
        turned = jnp.concatenate(gated, axis=0).T.astype(BF16)
        turned = jnp.concatenate([turned[:QR], turned[QR:]], axis=1)
        out_ref[m] = jnp.dot(turned, wo_ref[...], preferred_element_type=F32).astype(BF16)

    attended = []
    keys, values = project(0)
    scores, held = score(0, keys), values
    keys, values = project(1)
    for m in range(COLS):
        if m + 1 < COLS:
            following, after = score(m + 1, keys), values
        if m + 2 < COLS:
            keys, values = project(m + 2)
        highest = jnp.max(scores, axis=0, keepdims=True)
        attended.append(gather(jnp.exp2((scores - highest) * factor), held))
        if m + 1 < COLS:
            scores, held = following, after
    for m in range(COLS):
        finish(m, *attended[m])


def attend(k0, v0, far, other, wk, wv, masked, gates, bias, wo):
    return pl.pallas_call(
        attend_kernel,
        in_specs=[VMEM] * 10,
        out_specs=VMEM,
        out_shape=jax.ShapeDtypeStruct((COLS, QR, C), BF16),
        compiler_params=params(40),
        cost_estimate=pl.CostEstimate(
            flops=COLS * 8 * N * N * C, bytes_accessed=12 * N * N, transcendentals=COLS * N * N
        ),
        name="attend",
    )(k0, v0, far, other, wk, wv, masked, gates, bias, wo)


def local(pair, ln_gain, ln_shift, w_project, w_bias, w_out):
    swap_heads = functools.partial(lax.ppermute, axis_name="h", perm=[(0, 1), (1, 0)])
    swap_cores = functools.partial(lax.ppermute, axis_name="c", perm=[(0, 1), (1, 0)])
    where = [lax.axis_index(name) for name in ("h", "c", "y", "xl", "z")]
    where = jnp.stack(where).astype(jnp.int32)
    norm = jnp.stack([ln_gain, ln_shift])

    w_own = jnp.pad(w_bias.T, ((0, 14), (0, 0)))
    w_other = swap_heads(w_own)
    laid, picked = lay_out(where, pair, norm)
    blocks = pack(where, laid, picked, swap_cores(pair), norm, w_own, w_other)
    arrived = lax.all_to_all(blocks, CHIP, 0, 0, tiled=True)
    weights = jnp.concatenate([w_project.reshape(C, 4 * 64), w_out.T], axis=1)
    weights_other = swap_heads(weights)
    full = [
        jnp.concatenate([weights[:, t * 64 : (t + 1) * 64], weights_other[:, t * 64 : (t + 1) * 64]], axis=1)
        for t in range(5)
    ]
    wo = full[4].T.reshape(2, 2, DH, C).transpose(1, 0, 2, 3).reshape(C, C)
    full = (full[1], full[2].T, full[0].T, full[3].T, wo)
    arrived, *full = lax.optimization_barrier((arrived, *full))

    wk, wv, wq, wg, wo = full
    share, own = unpack(arrived)
    far = swap_heads(own)
    parts = [share] + [lax.ppermute(share, "y", [(i, (i + o) % 4) for i in range(4)]) for o in (1, 2, 3)]
    masked, gates = ask(own, wq, wg)
    k0, v0 = project(own, swap_cores(own), wk, wv)
    bias = place_bias(where, norm, w_own, w_other, share, 0, None)
    waited = (parts[3], masked, gates, k0, v0, bias)
    parts[3], masked, gates, k0, v0, bias = lax.optimization_barrier(waited)
    for step in (3, 2):
        bias = place_bias(where, norm, w_own, w_other, parts[step], step, bias)
    far, parts[1], bias = lax.optimization_barrier((far, parts[1], bias))
    far_other = swap_cores(far)
    bias = place_bias(where, norm, w_own, w_other, parts[1], 1, bias)
    done = attend(k0, v0, far, far_other, wk, wv, masked, gates, bias, wo)

    sent = done.reshape(COLS, 3, CHIPS, C).transpose(2, 0, 1, 3).reshape(CHIPS, 9, 4, C)
    returned = lax.all_to_all(sent, CHIP, 0, 0, tiled=True)
    return returned.reshape(N, 3, C).transpose(1, 0, 2)


def solution(mesh):
    fine = Mesh(mesh.devices.reshape(2, 4, 8, 2, 2), DAP + ("h",))
    in_specs = (P(DAP, None, None), P(), P(), P(None, None, "h"), P(None, "h"), P("h", None))
    out_specs = P(DAP + ("h",), None, None)
    return jax.shard_map(local, mesh=fine, in_specs=in_specs, out_specs=out_specs, check_vma=False)
```
